128 devices in a mesh: rows: 16 (over z, x_hi, core), cols: 8 (over x_lo, y).
Axes of the slice: x: 4 (x_hi: 2, x_lo: 2; x = x_hi * 2 + x_lo), y: 4, z: 4, core: 2. Of those that a mesh axis runs over, the one named last changes fastest.
Arguments:
- slm_field: float32 [2, 4096, 2048], P(None, 'rows', 'cols'), may hold values from -6 to 6
- target_light: float32 [32, 16, 256], P('rows', 'cols'), may hold values from 0 to 0.5
Outputs:
- gradient: float32 [2, 4096, 2048], P(None, 'rows', 'cols')
- light_field: float32 [32, 16, 256], P('rows', 'cols')
The draws below stay inside these ranges and needn't reach their ends.
All inputs are finite; a program needn't handle non-finite values.
Results may differ from the reference program's by a relative error of at most 0.012.
Values may be sent and summed in bfloat16 or wider, within the bound.
A program may use at most 64 MiB of HBM per device.

```python
import math
import jax
import jax.numpy as jnp
from jax import lax

WIN = 256
VIEWS = 16
STRIDE = 128
BIN = 16
FIELD_ROWS = 4096
FIELD_COLS = 2048
HOGEL_ROWS = 32
HOGEL_COLS = 16


def levels(key, dims, split, smallest, high):
    loudness, own = 1.0, jax.random.fold_in(key, 6)
    for dim, shards_of in split:
        draws = jnp.exp(jax.random.uniform(jax.random.fold_in(own, dim), (shards_of,), jnp.float32, smallest / len(split), high / len(split)))
        loudness = loudness * jnp.repeat(draws, dims[dim] // shards_of).reshape([-1 if axis == dim else 1 for axis in range(len(dims))])
    return loudness


def normal_values(key, shape, deviation, bound, shards=(), held_as=jnp.bfloat16):
    level = levels(key, shape, shards, -0.22, 0.18) if shards else 1.0
    drawn = jax.random.normal(key, shape, jnp.float32) * deviation * level
    return jnp.minimum(jnp.maximum(drawn, -bound), bound).astype(held_as)


def setup_inputs(seed: int = 0) -> dict:
    arg_keys = jax.random.split(jax.random.key(seed), 3)
    return {
        "slm_field": normal_values(arg_keys[0], (2, FIELD_ROWS, FIELD_COLS), 1.0, 6.0, ((1, 16), (2, 8)), jnp.float32),
        "target_light": jnp.clip(0.5 * jax.random.uniform(arg_keys[1], (HOGEL_ROWS, HOGEL_COLS, VIEWS * VIEWS), jnp.float32) ** levels(arg_keys[1], (HOGEL_ROWS, HOGEL_COLS, VIEWS * VIEWS), ((0, 16), (1, 8)), -0.2, 0.2), 0.0, 0.5),
    }


distance_px = 16000.0
index_ratio = 15.0

def freq_of(positions, count):
    return ((positions + count // 2) % count - count // 2).astype(jnp.float32) / count

def phase_of(freq_rows, freq_cols):
    radial = freq_rows * freq_rows + freq_cols * freq_cols
    return -2.0 * math.pi * distance_px * radial / (jnp.sqrt(index_ratio * index_ratio - radial) + index_ratio)

def hogel_tables():
    positions = jnp.arange(WIN, dtype=jnp.int32)
    tapers = jnp.sin(math.pi * (positions.astype(jnp.float32) + 0.5) / WIN) ** 2
    angles = -2.0 * math.pi / WIN * (positions[:, None] * positions[None, :] % WIN).astype(jnp.float32)
    cosine = tapers[:, None] * jnp.cos(angles)
    sine_part = tapers[:, None] * jnp.sin(angles)
    return (cosine.astype(jnp.bfloat16), sine_part.astype(jnp.bfloat16), (cosine / WIN).astype(jnp.bfloat16), (sine_part / WIN).astype(jnp.bfloat16))

def complex_product(pattern, left_re, left_im, right_re, right_im):

    def multiply(first, second):
        return jnp.einsum(pattern, first.astype(jnp.float32), second.astype(jnp.float32), precision=lax.Precision.HIGHEST)
    return (multiply(left_re, right_re) - multiply(left_im, right_im), multiply(left_re, right_im) + multiply(left_im, right_re))

def propagate(values, phase_sign):
    spectrum = jnp.fft.fft2(lax.complex(values[0], values[1]))
    freq_rows = freq_of(jnp.arange(FIELD_ROWS, dtype=jnp.int32), FIELD_ROWS)[:, None]
    freq_cols = freq_of(jnp.arange(FIELD_COLS, dtype=jnp.int32), FIELD_COLS)[None, :]
    phase = phase_of(freq_rows, freq_cols)
    kernel = lax.complex(jnp.cos(phase), phase_sign * jnp.sin(phase))
    result = jnp.fft.ifft2(spectrum * kernel)
    return jnp.stack([jnp.real(result), jnp.imag(result)])

def inner_forward(padded, col_re, col_im):
    count = padded.shape[1]
    hogels = padded.shape[2] // STRIDE - 1
    halves = padded.reshape(2, count, hogels + 1, STRIDE)
    windows = jnp.concatenate([halves[:, :, :-1], halves[:, :, 1:]], axis=3)
    lines_re, lines_im = complex_product('xjc,cq->xjq', windows[0], windows[1], col_re, col_im)
    return jnp.stack([lines_re, lines_im]).astype(jnp.bfloat16)

def hogel_step(window_rows, goal_rows, row_re, row_im):
    hogels = window_rows.shape[2]
    spec_re, spec_im = complex_product('rp,rjq->jpq', row_re, row_im, window_rows[0], window_rows[1])
    power = spec_re * spec_re + spec_im * spec_im
    light_row = power.reshape(hogels, VIEWS, BIN, VIEWS, BIN).sum(axis=(2, 4)) / (BIN * BIN)
    weights = 4.0 * (light_row - goal_rows.reshape(hogels, VIEWS, VIEWS))
    spread = jnp.broadcast_to(weights[:, :, None, :, None], (hogels, VIEWS, BIN, VIEWS, BIN)).reshape(hogels, WIN, WIN)
    weighted_re = (spread * spec_re).astype(jnp.bfloat16)
    weighted_im = (spread * spec_im).astype(jnp.bfloat16)
    back_re, back_im = complex_product('rp,jpq->rjq', row_re, -row_im, weighted_re, weighted_im)
    return (light_row.reshape(hogels, VIEWS * VIEWS), back_re, back_im)

def inner_adjoint(block, col_re, col_im):
    spread_re, spread_im = complex_product('xjq,cq->xjc', block[0], block[1], col_re, -col_im)
    spread = jnp.stack([spread_re, spread_im])
    first_half = spread[..., :STRIDE]
    second_half = spread[..., STRIDE:]
    joined = first_half + jnp.roll(second_half, 1, axis=2)
    return joined.reshape(2, block.shape[1], -1)

def reference(slm_field, target_light):
    col_re, col_im, row_re, row_im = hogel_tables()
    near_field = propagate(slm_field, 1.0).astype(jnp.bfloat16)
    padded = jnp.concatenate([near_field, near_field[:, :, :STRIDE]], axis=2)
    bands = padded.reshape(2, HOGEL_ROWS, STRIDE, FIELD_COLS + STRIDE).transpose(1, 0, 2, 3)
    spectra = lax.map(lambda band_data: inner_forward(band_data, col_re, col_im), bands)

    def hogel_row(pending, position):
        upper = lax.dynamic_index_in_dim(spectra, position, 0, keepdims=False)
        lower = lax.dynamic_index_in_dim(spectra, (position + 1) % HOGEL_ROWS, 0, keepdims=False)
        window_rows = jnp.concatenate([upper, lower], axis=1)
        goal_rows = lax.dynamic_index_in_dim(target_light, position, 0, keepdims=False)
        light_row, back_re, back_im = hogel_step(window_rows, goal_rows, row_re, row_im)
        returned = jnp.stack([back_re, back_im])
        return (returned[:, STRIDE:], (light_row, returned[:, :STRIDE] + pending))
    start = jnp.zeros((2, STRIDE, HOGEL_COLS, WIN), jnp.float32)
    last, (lights, blocks) = lax.scan(hogel_row, start, jnp.arange(HOGEL_ROWS, dtype=jnp.int32))
    blocks = blocks.at[0].add(last)
    back_lines = blocks.astype(jnp.bfloat16)
    rows_back = lax.map(lambda block: inner_adjoint(block, col_re, col_im), back_lines)
    back_near = rows_back.transpose(1, 0, 2, 3).reshape(2, FIELD_ROWS, FIELD_COLS)
    gradient = propagate(back_near, -1.0)
    return (gradient, lights)
```

```python
import functools
import math

import jax
import jax.numpy as jnp
import numpy as np
from jax import lax
from jax.experimental import pallas as pl
from jax.experimental.pallas import tpu as pltpu
from jax.sharding import PartitionSpec as P

MESH = pl.DeviceIdType.MESH

f32, bf16 = jnp.float32, jnp.bfloat16

def mm(a, b, dims=((1,), (0,))):
    return lax.dot_general(a, b, (dims, ((), ())), preferred_element_type=f32)

def roll(x, shift):
    return pltpu.roll(x, shift, x.ndim - 1)

def turn(pair, angle):
    re, im = pair
    c, s = math.cos(angle), math.sin(angle)
    if abs(s) < 1e-9:
        return (re, im) if c > 0 else (-re, -im)
    if abs(c) < 1e-9:
        return (-im, re) if s > 0 else (im, -re)
    if abs(abs(c) - abs(s)) < 1e-9:
        k = abs(c)
        a, b = (re, im) if c > 0 else (-re, -im)
        if (s > 0) == (c > 0):
            return k * (a - b), k * (a + b)
        return k * (a + b), k * (b - a)
    return re * c - im * s, re * s + im * c

def fft_list(xs, sign):
    n = len(xs)
    if n == 1:
        return list(xs)
    even, odd = fft_list(xs[0::2], sign), fft_list(xs[1::2], sign)
    out = [None] * n
    for k in range(n // 2):
        t = turn(odd[k], sign * 2 * math.pi * k / n)
        e = even[k]
        out[k] = (e[0] + t[0], e[1] + t[1])
        out[k + n // 2] = (e[0] - t[0], e[1] - t[1])
    return out

def real_fft8(x):
    s = math.sqrt(0.5)
    a0, a1 = x[0] + x[4], x[0] - x[4]
    b0, b1 = x[2] + x[6], x[2] - x[6]
    c0, c1 = x[1] + x[5], x[1] - x[5]
    d0, d1 = x[3] + x[7], x[3] - x[7]
    e1, f1 = s * (c1 - d1), s * (c1 + d1)
    r1, r3 = a1 + e1, a1 - e1
    i1, i3 = -(b1 + f1), b1 - f1
    r2, i2 = a0 - b0, d0 - c0
    p, q = a0 + b0, c0 + d0
    return [(p + q, None), (r1, i1), (r2, i2), (r3, i3), (p - q, None), (r3, -i3), (r2, -i2), (r1, -i1)]

def lane_swap(xs):
    lane = lax.broadcasted_iota(jnp.int32, xs[0].shape, xs[0].ndim - 1)
    for step, (pairs, width) in enumerate((( ((0, 1), (2, 3)), 32), (((0, 2), (1, 3)), 64))):
        low = (lane // width) % 2 == 0
        out = [None] * 4
        for lo, hi in pairs:
            out[lo] = jnp.where(low, xs[lo], roll(xs[hi], width))
            out[hi] = jnp.where(low, roll(xs[lo], 128 - width), xs[hi])
        xs = out
    return xs

def by_i(x):
    lane = lax.broadcasted_iota(jnp.int32, x.shape, x.ndim - 1)
    return jnp.where(lane < 64, -1.0, 1.0) * roll(x, 64)

def tables():
    a = np.arange(256)
    t256 = 2 * np.pi * ((a[:, None] * a[None]) % 256) / 256
    C, S = np.cos(t256), np.sin(t256)
    cs = np.concatenate([C, S], 1)
    b = np.arange(128)
    t128 = 2 * np.pi * ((b[:, None] * b[None]) % 128) / 128
    c1, s1 = np.cos(t128), np.sin(t128)
    dfwd = np.block([[c1, -s1], [s1, c1]])
    dinv = np.block([[c1, s1], [-s1, c1]])
    taper = np.sin(np.pi * (a + 0.5) / 256) ** 2
    tr = taper[:, None] * C
    ti = -taper[:, None] * S
    rr, rim = tr / 256, ti / 256
    row = np.zeros((2, 256, 4, 2, 64))
    for g in range(4):
        s = slice(64 * g, 64 * g + 64)
        row[0, :, g, 0], row[0, :, g, 1] = rr[:, s], rim[:, s]
        row[1, :, g, 0], row[1, :, g, 1] = -rim[:, s], rr[:, s]
    row = row.reshape(512, 512)
    ct = np.concatenate([tr.T, ti.T], 1)
    cth = np.concatenate([tr, ti], 1)
    v0 = np.arange(8)
    th = 2 * np.pi * v0[:, None] * a[None] / 2048
    u0 = np.arange(32)
    t4 = 2 * np.pi * u0[:, None] * b[None] / 4096
    l = np.arange(128)
    ones = ((l[:, None] % 64) // 16 == (l[None] % 64) // 16) / 256.0
    B = lambda x: x.astype(jnp.bfloat16)
    F = lambda x: x.astype(np.float32)
    return dict(cs=B(cs), dfwd=B(dfwd), dinv=B(dinv), row=B(row), rowh=B(row.T.copy()), ct=B(ct), cth=B(cth),
                tw=F(np.stack([np.cos(th), np.sin(th)])),
                twl=F(np.broadcast_to(np.stack([np.cos(th), np.sin(th)])[..., None], (2, 8, 256, 128))),
                t4=F(np.stack([np.cos(t4), np.sin(t4)])), ones=B(ones))

def filt(me):
    q, k = me // 32, me % 32
    u0 = lax.broadcasted_iota(jnp.int32, (32, 16, 128), 0)
    w = lax.broadcasted_iota(jnp.int32, (32, 16, 128), 1)
    u1 = lax.broadcasted_iota(jnp.int32, (32, 16, 128), 2)
    u = 32 * u1 + u0
    v = 8 * (8 * k + w % 8) + 2 * q + w // 8
    fx = jnp.where(u < 2048, u, u - 4096).astype(f32) / 4096
    fy = jnp.where(v < 1024, v, v - 2048).astype(f32) / 2048
    s = fx * fx + fy * fy
    turns = 16000.0 * s / (jnp.sqrt(225.0 - s) + 15.0)
    quarters = 4.0 * (turns - jnp.floor(turns))
    nearest = jnp.floor(quarters + 0.5)
    z = (quarters - nearest) * (math.pi / 2)
    n = nearest.astype(jnp.int32)
    zz = z * z
    sine = z * (1 + zz * (-1 / 6 + zz * (1 / 120 + zz * (-1 / 5040 + zz / 362880))))
    cosine = 1 + zz * (-1 / 2 + zz * (1 / 24 + zz * (-1 / 720 + zz / 40320)))
    odd = n % 2 == 1
    c, d = jnp.where(odd, sine, cosine), jnp.where(odd, cosine, sine)
    half = 2.0 ** -23
    c = jnp.where((n % 4 == 1) | (n % 4 == 2), -half, half) * c
    d = jnp.where(n % 4 >= 2, half, -half) * d
    return c.reshape(512, 128), d.reshape(512, 128)

def stage_a(x, T):
    z = fft_list([(x[c, 0], x[c, 1]) for c in range(8)], -1)
    rows = []
    zz = []
    for v in range(8):
        c, s = T["tw"][0, v:v + 1], T["tw"][1, v:v + 1]
        re, im = z[v]
        zz.append((re * c + im * s, im * c - re * s) if v else (re, im))
    for q in range(4):
        for v in (2 * q, 2 * q + 1):
            rows.append(jnp.concatenate([zz[v][0], zz[v][1]], 1).astype(bf16))
        for v in (2 * q, 2 * q + 1):
            rows.append(jnp.concatenate([zz[v][1], -zz[v][0]], 1).astype(bf16))
    y = mm(T["cs"][...], jnp.concatenate(rows, 0), ((1,), (1,)))
    return [y[:, 128 * q:128 * q + 128].reshape(32, 8, 128) for q in range(4)]

def columns(xs, T, kr, ki, sign):
    z = fft_list(xs, -1)
    lhs = []
    for u in range(32):
        c, s = T["t4"][0, u:u + 1], T["t4"][1, u:u + 1]
        re, im = z[u]
        lhs.append(jnp.concatenate([re * c + im * s, im * c - re * s], 1).astype(bf16))
    f = mm(jnp.concatenate(lhs, 0), T["dfwd"][...])
    fr, fi = f[:, :128], f[:, 128:]
    if sign > 0:
        pr, pi = fr * kr - fi * ki, fr * ki + fi * kr
    else:
        pr, pi = fr * kr + fi * ki, fi * kr - fr * ki
    g = mm(jnp.concatenate([pr, pi], 1).astype(bf16), T["dinv"][...])
    ys = []
    for u in range(32):
        c, s = T["t4"][0, u:u + 1], T["t4"][1, u:u + 1]
        re, im = g[16 * u:16 * u + 16, :128], g[16 * u:16 * u + 16, 128:]
        ys.append((re * c - im * s, im * c + re * s))
    return fft_list(ys, 1)

def stage_b(r2, T, kr, ki):
    b = lane_swap([r2[:, g] for g in range(4)])
    xs = [(jnp.concatenate([b[0][i], b[1][i]], 0), jnp.concatenate([b[2][i], b[3][i]], 0)) for i in range(32)]
    n = columns(xs, T, kr, ki, 1)
    n = [(re.astype(bf16), im.astype(bf16)) for re, im in n]
    lhs = jnp.concatenate([jnp.concatenate([n[i][0], n[(i + 1) % 32][0], n[i][1], n[(i + 1) % 32][1]], 1) for i in range(32)], 0)
    o = mm(lhs, T["row"][...])
    return [o[:, 128 * g:128 * g + 128].reshape(32, 16, 128).astype(bf16) for g in range(4)]

def stage_c(r3, target, T):
    x = r3.astype(f32).reshape(4, 32, 2, 8, 128)
    cols = []
    for v in range(8):
        xv = x[v // 2, :, v % 2].reshape(256, 128)
        cols.append(jnp.concatenate([xv.astype(bf16), by_i(xv).astype(bf16)], 0))
    o = mm(T["cs"][...], jnp.concatenate(cols, 1))
    ps = []
    for v in range(8):
        zv = o[:, 128 * v:128 * v + 128]
        ps.append((zv * T["twl"][0, v], zv * T["twl"][1, v]))
    near = [p + by_i(q) for p, q in fft_list(ps, 1)]
    nb = [n.astype(bf16) for n in near]
    jb = [by_i(n).astype(bf16) for n in near]
    spec = []
    for j in range(16):
        c, d = j // 2, (j // 2 + 1) % 8
        if j % 2 == 0:
            rhs = jnp.concatenate([nb[c], jb[c]], 0)
        else:
            rhs = jnp.concatenate([nb[c][128:], nb[d][:128], jb[c][128:], jb[d][:128]], 0)
        spec.append(mm(T["ct"][...], rhs))
    sums = jnp.concatenate([(s * s).reshape(16, 16, 128).sum(1) for s in spec], 0)
    hi = sums.astype(bf16)
    lo = (sums - hi.astype(f32)).astype(bf16)
    light = mm(hi, T["ones"][...]) + mm(lo, T["ones"][...])
    wt = 4.0 * (light - target)
    back = []
    for j in range(16):
        w = spec[j] * jnp.concatenate([jnp.broadcast_to(wt[r:r + 1], (16, 128)) for r in range(16 * j, 16 * j + 16)], 0)
        back.append(mm(T["cth"][...], jnp.concatenate([w.astype(bf16), (-by_i(w)).astype(bf16)], 0)))
    bn = []
    for c in range(8):
        e, o_, l = back[2 * c], back[2 * c + 1], back[(2 * c - 1) % 16]
        bn.append(jnp.concatenate([e[:128] + l[128:], o_[:128] + e[128:]], 0))
    cols = []
    for v, (e, f) in enumerate(real_fft8(bn)):
        c, s = T["twl"][0, v], T["twl"][1, v]
        if f is None:
            p, q = e * c, -e * s
        else:
            p, q = e * c + f * s, f * c - e * s
        h = p + by_i(q)
        cols.append(jnp.concatenate([h.astype(bf16), (-by_i(h)).astype(bf16)], 0))
    y = mm(T["cs"][...], jnp.concatenate(cols, 1))
    outs = []
    for q in range(4):
        a = y[:, 256 * q:256 * q + 128].reshape(32, 1, 8, 128)
        b = y[:, 256 * q + 128:256 * q + 256].reshape(32, 1, 8, 128)
        outs.append(jnp.concatenate([a, b], 1).reshape(32, 16, 128).astype(bf16))
    return outs, light

def stage_d(r4, T, kr, ki):
    lhs = jnp.concatenate([r4[:, g].reshape(512, 128) for g in range(4)], 1)
    o = mm(lhs, T["rowh"][...])
    xs = []
    for i in range(32):
        a, b = o[16 * i:16 * i + 16], o[16 * ((i - 1) % 32):16 * ((i - 1) % 32) + 16]
        xs.append((a[:, :128] + b[:, 128:256], a[:, 256:384] + b[:, 384:]))
    n = columns(xs, T, kr, ki, -1)
    parts = []
    for ri in range(2):
        for v in range(2):
            parts.append(jnp.stack([n[i][ri][8 * v:8 * v + 8] for i in range(32)], 0))
    return lane_swap(parts)

def stage_e(r5, T):
    x = jnp.concatenate([r5[q].reshape(256, 128).T for q in range(4)], 0).astype(bf16)
    o = mm(x, T["cs"][...])
    zs = []
    for v in range(8):
        b = 128 * (v // 2) + 32 * (v % 2)
        pr, pi = o[b:b + 32], o[b + 64:b + 96]
        re, im = pr[:, :256] - pi[:, 256:], pi[:, :256] + pr[:, 256:]
        if v:
            c, s = T["tw"][0, v:v + 1], T["tw"][1, v:v + 1]
            re, im = re * c - im * s, im * c + re * s
        zs.append((re, im))
    return fft_list(zs, 1)


NAMES = ("cs", "dfwd", "dinv", "row", "rowh", "ct", "cth", "tw", "twl", "t4", "ones", "spread", "pick")


def exact(x, table):
    hi = x.astype(bf16)
    rest = x - hi.astype(f32)
    mid = rest.astype(bf16)
    low = (rest - mid.astype(f32)).astype(bf16)
    return mm(hi, table) + mm(mid, table) + mm(low, table)


def body(field, target, *refs):
    n = len(NAMES)
    hbm, refs = dict(zip(NAMES, refs[:n])), refs[n:]
    grad, light_out = refs[:2]
    T, refs = dict(zip(NAMES, refs[2:2 + n])), refs[2 + n:]
    x1, r1, ts, tr, s2, r2, s3, r3, ls, lr, s4, r4, s5, r5, s6, r6, kr, ki, tsem, ssem, rsem = refs
    row, col = lax.axis_index("rows"), lax.axis_index("cols")
    me = row * 8 + col

    def place(d):
        return (d // 8, lax.rem(d, 8))

    loads = [pltpu.make_async_copy(hbm[k], T[k], tsem.at[i]) for i, k in enumerate(NAMES)]
    for copy in loads:
        copy.start()
    barrier = pltpu.get_barrier_semaphore()

    def greet(k, _):
        pl.semaphore_signal(barrier, inc=1, device_id=place(lax.rem(me + k, 128)), device_id_type=MESH)
        return 0

    lax.fori_loop(1, 128, greet, 0)

    def copy_to(src, dst, slot, d):
        return pltpu.make_async_remote_copy(src, dst, ssem.at[slot], rsem.at[slot], device_id=d, device_id_type=MESH)

    def send_cols(src, dst, slot):
        for k in range(1, 8):
            d = lax.rem(col + k, 8)
            copy_to(src.at[d], dst.at[col], slot, (row, d)).start()
        dst[pl.ds(col, 1)] = src[pl.ds(col, 1)]

    def send_all(src, dst, slot):
        def one(k, _):
            d = lax.rem(me + k, 128)
            copy_to(src.at[d], dst.at[me], slot, place(d)).start()
            return 0

        lax.fori_loop(1, 128, one, 0)
        dst[pl.ds(me, 1)] = src[pl.ds(me, 1)]

    def arrived(dst, slot):
        some = dst.at[pl.ds(0, dst.shape[0] - 1)]
        copy_to(some, some, slot, (row, col)).wait_recv()

    def sent(src, slot):
        some = src.at[pl.ds(0, src.shape[0] - 1)]
        copy_to(some, some, slot, (row, col)).wait_send()

    for c in range(8):
        x1[c] = field[:, 32 * c:32 * c + 32, :].astype(bf16)
    for copy in loads:
        copy.wait()
    lane = lax.broadcasted_iota(jnp.int32, (4, 16, 256), 2) % 16
    which = lax.broadcasted_iota(jnp.int32, (4, 16, 256), 1)
    chosen = jnp.where(lane == which, jnp.broadcast_to(target[...][:, None, :], (4, 16, 256)), 0.0)
    goals = exact(chosen.reshape(64, 256), T["spread"][...])
    for i in range(2):
        for g in range(4):
            ts[4 * i + g] = goals[32 * i:32 * i + 32, 128 * g:128 * g + 128]
    pl.semaphore_wait(barrier, 127)
    send_cols(x1, r1, 0)
    send_cols(ts, tr, 1)
    a, b = filt(me)
    kr[...] = a
    ki[...] = b
    arrived(r1, 0)
    for q, y in enumerate(stage_a(r1[...].astype(f32), T)):
        s2[32 * q:32 * q + 32] = y
    send_all(s2, r2, 2)
    arrived(r2, 2)
    for g, y in enumerate(stage_b(r2[...].reshape(32, 4, 8, 128), T, kr[...], ki[...])):
        for i in range(32):
            s3[4 * i + g] = y[i]
    send_all(s3, r3, 3)
    arrived(tr, 1)
    arrived(r3, 3)
    ys, light = stage_c(r3[...], tr[...].reshape(256, 128), T)
    for q, y in enumerate(ys):
        s4[32 * q:32 * q + 32] = y
    send_all(s4, r4, 4)
    ls[...] = light.reshape(8, 32, 128)
    send_cols(ls, lr, 5)
    arrived(r4, 4)
    for g, y in enumerate(stage_d(r4[...].reshape(32, 4, 16, 128), T, kr[...], ki[...])):
        for i in range(32):
            s5[4 * i + g] = y[i]
    send_all(s5, r5, 6)
    arrived(lr, 5)
    parts = [jnp.concatenate([lr[4 * i + g] for g in range(4)], 1) for i in range(2)]
    picked = exact(jnp.concatenate(parts, 0), T["pick"][...]).reshape(4, 16, 256)
    light_out[...] = jnp.where(lane == which, picked, 0.0).sum(1)
    arrived(r5, 6)
    for c, (re, im) in enumerate(stage_e(r5[...].reshape(4, 32, 8, 128), T)):
        s6[c, 0] = re.astype(bf16)
        s6[c, 1] = im.astype(bf16)
    send_cols(s6, r6, 7)
    arrived(r6, 7)
    for c in range(8):
        grad[:, 32 * c:32 * c + 32, :] = r6[c].astype(f32)
    for slot, src in enumerate((x1, ts, s2, s3, s4, ls, s5, s6)):
        sent(src, slot)


def local(slm_field, target_light):
    T = tables()
    a = np.arange(256) // 16
    lanes = np.arange(512)
    view = 4 * (lanes // 128) + (lanes % 64) // 16
    spread = a[:, None] == view[None]
    T["spread"] = spread.astype(jnp.bfloat16)
    T["pick"] = (spread & (lanes % 128 % 16 == 0) & (lanes % 128 < 64)).T.astype(jnp.bfloat16)
    consts = [jnp.asarray(T[k]) for k in NAMES]
    vmem, anywhere = pl.BlockSpec(memory_space=pltpu.VMEM), pl.BlockSpec(memory_space=pl.ANY)
    V = pltpu.VMEM
    wide, f_all, b_all = V((8, 2, 32, 256), bf16), V((128, 8, 128), f32), V((128, 16, 128), bf16)
    small = V((8, 32, 128), f32)
    gradient, light = pl.pallas_call(
        body,
        out_shape=(jax.ShapeDtypeStruct((2, 256, 256), f32), jax.ShapeDtypeStruct((4, 256), f32)),
        in_specs=[vmem, vmem] + [anywhere] * len(NAMES),
        out_specs=(vmem, vmem),
        scratch_shapes=[V(T[k].shape, T[k].dtype) for k in NAMES]
        + [wide, wide, small, small, f_all, f_all, b_all, b_all, small, small, b_all, b_all, f_all, f_all, wide, wide]
        + [V((512, 128), f32)] * 2
        + [pltpu.SemaphoreType.DMA((len(NAMES),)), pltpu.SemaphoreType.DMA((8,)), pltpu.SemaphoreType.DMA((8,))],
        compiler_params=pltpu.CompilerParams(collective_id=0, has_side_effects=True, vmem_limit_bytes=56 << 20),
    )(slm_field, target_light.reshape(4, 256), *consts)
    return gradient, light.reshape(2, 2, 256)


def solution(mesh):
    return jax.shard_map(
        local,
        mesh=mesh,
        in_specs=(P(None, "rows", "cols"), P("rows", "cols", None)),
        out_specs=(P(None, "rows", "cols"), P("rows", "cols", None)),
        check_vma=False,
    )
```

```python
import functools
import math

import jax
import jax.numpy as jnp
import numpy as np
from jax import lax
from jax.experimental import pallas as pl
from jax.experimental.pallas import tpu as pltpu
from jax.sharding import PartitionSpec as P

MESH = pl.DeviceIdType.MESH

f32, bf16 = jnp.float32, jnp.bfloat16

def mm(a, b, dims=((1,), (0,))):
    return lax.dot_general(a, b, (dims, ((), ())), preferred_element_type=f32)

def roll(x, shift):
    return pltpu.roll(x, shift, x.ndim - 1)

def turn(pair, angle):
    re, im = pair
    c, s = math.cos(angle), math.sin(angle)
    if abs(s) < 1e-9:
        return (re, im) if c > 0 else (-re, -im)
    if abs(c) < 1e-9:
        return (-im, re) if s > 0 else (im, -re)
    if abs(abs(c) - abs(s)) < 1e-9:
        k = abs(c)
        a, b = (re, im) if c > 0 else (-re, -im)
        if (s > 0) == (c > 0):
            return k * (a - b), k * (a + b)
        return k * (a + b), k * (b - a)
    return re * c - im * s, re * s + im * c

def fft_list(xs, sign):
    n = len(xs)
    if n == 1:
        return list(xs)
    even, odd = fft_list(xs[0::2], sign), fft_list(xs[1::2], sign)
    out = [None] * n
    for k in range(n // 2):
        t = turn(odd[k], sign * 2 * math.pi * k / n)
        e = even[k]
        out[k] = (e[0] + t[0], e[1] + t[1])
        out[k + n // 2] = (e[0] - t[0], e[1] - t[1])
    return out

def real_fft8(x):
    s = math.sqrt(0.5)
    a0, a1 = x[0] + x[4], x[0] - x[4]
    b0, b1 = x[2] + x[6], x[2] - x[6]
    c0, c1 = x[1] + x[5], x[1] - x[5]
    d0, d1 = x[3] + x[7], x[3] - x[7]
    e1, f1 = s * (c1 - d1), s * (c1 + d1)
    r1, r3 = a1 + e1, a1 - e1
    i1, i3 = -(b1 + f1), b1 - f1
    r2, i2 = a0 - b0, d0 - c0
    p, q = a0 + b0, c0 + d0
    return [(p + q, None), (r1, i1), (r2, i2), (r3, i3), (p - q, None), (r3, -i3), (r2, -i2), (r1, -i1)]

def lane_swap(xs):
    lane = lax.broadcasted_iota(jnp.int32, xs[0].shape, xs[0].ndim - 1)
    for step, (pairs, width) in enumerate((( ((0, 1), (2, 3)), 32), (((0, 2), (1, 3)), 64))):
        low = (lane // width) % 2 == 0
        out = [None] * 4
        for lo, hi in pairs:
            out[lo] = jnp.where(low, xs[lo], roll(xs[hi], width))
            out[hi] = jnp.where(low, roll(xs[lo], 128 - width), xs[hi])
        xs = out
    return xs

def by_i(x):
    lane = lax.broadcasted_iota(jnp.int32, x.shape, x.ndim - 1)
    return jnp.where(lane < 64, -1.0, 1.0) * roll(x, 64)

def tables():
    a = np.arange(256)
    t256 = 2 * np.pi * ((a[:, None] * a[None]) % 256) / 256
    C, S = np.cos(t256), np.sin(t256)
    cs = np.concatenate([C, S], 1)
    b = np.arange(128)
    t128 = 2 * np.pi * ((b[:, None] * b[None]) % 128) / 128
    c1, s1 = np.cos(t128), np.sin(t128)
    dfwd = np.block([[c1, -s1], [s1, c1]])
    dinv = np.block([[c1, s1], [-s1, c1]])
    taper = np.sin(np.pi * (a + 0.5) / 256) ** 2
    tr = taper[:, None] * C
    ti = -taper[:, None] * S
    rr, rim = tr / 256, ti / 256
    row = np.zeros((2, 256, 4, 2, 64))
    for g in range(4):
        s = slice(64 * g, 64 * g + 64)
        row[0, :, g, 0], row[0, :, g, 1] = rr[:, s], rim[:, s]
        row[1, :, g, 0], row[1, :, g, 1] = -rim[:, s], rr[:, s]
    row = row.reshape(512, 512)
    ct = np.concatenate([tr.T, ti.T], 1)
    cth = np.concatenate([tr, ti], 1)
    v0 = np.arange(8)
    th = 2 * np.pi * v0[:, None] * a[None] / 2048
    u0 = np.arange(32)
    t4 = 2 * np.pi * u0[:, None] * b[None] / 4096
    l = np.arange(128)
    ones = ((l[:, None] % 64) // 16 == (l[None] % 64) // 16) / 256.0
    B = lambda x: x.astype(jnp.bfloat16)
    F = lambda x: x.astype(np.float32)
    return dict(cs=B(cs), dfwd=B(dfwd), dinv=B(dinv), row=B(row), rowh=B(row.T.copy()), ct=B(ct), cth=B(cth),
                tw=F(np.stack([np.cos(th), np.sin(th)])),
                twl=F(np.broadcast_to(np.stack([np.cos(th), np.sin(th)])[..., None], (2, 8, 256, 128))),
                t4=F(np.stack([np.cos(t4), np.sin(t4)])), ones=B(ones))

def filt(me):
    q, k = me // 32, me % 32
    u0 = lax.broadcasted_iota(jnp.int32, (32, 16, 128), 0)
    w = lax.broadcasted_iota(jnp.int32, (32, 16, 128), 1)
    u1 = lax.broadcasted_iota(jnp.int32, (32, 16, 128), 2)
    u = 32 * u1 + u0
    v = 8 * (8 * k + w % 8) + 2 * q + w // 8
    fx = jnp.where(u < 2048, u, u - 4096).astype(f32) / 4096
    fy = jnp.where(v < 1024, v, v - 2048).astype(f32) / 2048
    s = fx * fx + fy * fy
    turns = 16000.0 * s / (jnp.sqrt(225.0 - s) + 15.0)
    quarters = 4.0 * (turns - jnp.floor(turns))
    nearest = jnp.floor(quarters + 0.5)
    z = (quarters - nearest) * (math.pi / 2)
    n = nearest.astype(jnp.int32)
    zz = z * z
    sine = z * (1 + zz * (-1 / 6 + zz * (1 / 120 + zz * (-1 / 5040 + zz / 362880))))
    cosine = 1 + zz * (-1 / 2 + zz * (1 / 24 + zz * (-1 / 720 + zz / 40320)))
    odd = n % 2 == 1
    c, d = jnp.where(odd, sine, cosine), jnp.where(odd, cosine, sine)
    half = 2.0 ** -23
    c = jnp.where((n % 4 == 1) | (n % 4 == 2), -half, half) * c
    d = jnp.where(n % 4 >= 2, half, -half) * d
    return c.reshape(512, 128), d.reshape(512, 128)

def stage_a(x, T):
    z = fft_list([(x[c, 0], x[c, 1]) for c in range(8)], -1)
    rows = []
    zz = []
    for v in range(8):
        c, s = T["tw"][0, v:v + 1], T["tw"][1, v:v + 1]
        re, im = z[v]
        zz.append((re * c + im * s, im * c - re * s) if v else (re, im))
    for q in range(4):
        for v in (2 * q, 2 * q + 1):
            rows.append(jnp.concatenate([zz[v][0], zz[v][1]], 1).astype(bf16))
        for v in (2 * q, 2 * q + 1):
            rows.append(jnp.concatenate([zz[v][1], -zz[v][0]], 1).astype(bf16))
    y = mm(T["cs"][...], jnp.concatenate(rows, 0), ((1,), (1,)))
    return [y[:, 128 * q:128 * q + 128].reshape(32, 8, 128) for q in range(4)]

def columns(xs, T, kr, ki, sign):
    z = fft_list(xs, -1)
    lhs = []
    for u in range(32):
        c, s = T["t4"][0, u:u + 1], T["t4"][1, u:u + 1]
        re, im = z[u]
        lhs.append(jnp.concatenate([re * c + im * s, im * c - re * s], 1).astype(bf16))
    f = mm(jnp.concatenate(lhs, 0), T["dfwd"][...])
    fr, fi = f[:, :128], f[:, 128:]
    if sign > 0:
        pr, pi = fr * kr - fi * ki, fr * ki + fi * kr
    else:
        pr, pi = fr * kr + fi * ki, fi * kr - fr * ki
    g = mm(jnp.concatenate([pr, pi], 1).astype(bf16), T["dinv"][...])
    ys = []
    for u in range(32):
        c, s = T["t4"][0, u:u + 1], T["t4"][1, u:u + 1]
        re, im = g[16 * u:16 * u + 16, :128], g[16 * u:16 * u + 16, 128:]
        ys.append((re * c - im * s, im * c + re * s))
    return fft_list(ys, 1)

def stage_b(r2, T, kr, ki):
    b = lane_swap([r2[:, g] for g in range(4)])
    xs = [(jnp.concatenate([b[0][i], b[1][i]], 0), jnp.concatenate([b[2][i], b[3][i]], 0)) for i in range(32)]
    n = columns(xs, T, kr, ki, 1)
    n = [(re.astype(bf16), im.astype(bf16)) for re, im in n]
    lhs = jnp.concatenate([jnp.concatenate([n[i][0], n[(i + 1) % 32][0], n[i][1], n[(i + 1) % 32][1]], 1) for i in range(32)], 0)
    o = mm(lhs, T["row"][...])
    return [o[:, 128 * g:128 * g + 128].reshape(32, 16, 128).astype(bf16) for g in range(4)]

def stage_c(r3, target, T):
    x = r3.astype(f32).reshape(4, 32, 2, 8, 128)
    cols = []
    for v in range(8):
        xv = x[v // 2, :, v % 2].reshape(256, 128)
        cols.append(jnp.concatenate([xv.astype(bf16), by_i(xv).astype(bf16)], 0))
    o = mm(T["cs"][...], jnp.concatenate(cols, 1))
    ps = []
    for v in range(8):
        zv = o[:, 128 * v:128 * v + 128]
        ps.append((zv * T["twl"][0, v], zv * T["twl"][1, v]))
    near = [p + by_i(q) for p, q in fft_list(ps, 1)]
    nb = [n.astype(bf16) for n in near]
    jb = [by_i(n).astype(bf16) for n in near]
    spec = []
    for j in range(16):
        c, d = j // 2, (j // 2 + 1) % 8
        if j % 2 == 0:
            rhs = jnp.concatenate([nb[c], jb[c]], 0)
        else:
            rhs = jnp.concatenate([nb[c][128:], nb[d][:128], jb[c][128:], jb[d][:128]], 0)
        spec.append(mm(T["ct"][...], rhs))
    sums = jnp.concatenate([(s * s).reshape(16, 16, 128).sum(1) for s in spec], 0)
    hi = sums.astype(bf16)
    lo = (sums - hi.astype(f32)).astype(bf16)
    light = mm(hi, T["ones"][...]) + mm(lo, T["ones"][...])
    wt = 4.0 * (light - target)
    back = []
    for j in range(16):
        w = spec[j] * jnp.concatenate([jnp.broadcast_to(wt[r:r + 1], (16, 128)) for r in range(16 * j, 16 * j + 16)], 0)
        back.append(mm(T["cth"][...], jnp.concatenate([w.astype(bf16), (-by_i(w)).astype(bf16)], 0)))
    bn = []
    for c in range(8):
        e, o_, l = back[2 * c], back[2 * c + 1], back[(2 * c - 1) % 16]
        bn.append(jnp.concatenate([e[:128] + l[128:], o_[:128] + e[128:]], 0))
    cols = []
    for v, (e, f) in enumerate(real_fft8(bn)):
        c, s = T["twl"][0, v], T["twl"][1, v]
        if f is None:
            p, q = e * c, -e * s
        else:
            p, q = e * c + f * s, f * c - e * s
        h = p + by_i(q)
        cols.append(jnp.concatenate([h.astype(bf16), (-by_i(h)).astype(bf16)], 0))
    y = mm(T["cs"][...], jnp.concatenate(cols, 1))
    outs = []
    for q in range(4):
        a = y[:, 256 * q:256 * q + 128].reshape(32, 1, 8, 128)
        b = y[:, 256 * q + 128:256 * q + 256].reshape(32, 1, 8, 128)
        outs.append(jnp.concatenate([a, b], 1).reshape(32, 16, 128).astype(bf16))
    return outs, light

def stage_d(r4, T, kr, ki):
    lhs = jnp.concatenate([r4[:, g].reshape(512, 128) for g in range(4)], 1)
    o = mm(lhs, T["rowh"][...])
    xs = []
    for i in range(32):
        a, b = o[16 * i:16 * i + 16], o[16 * ((i - 1) % 32):16 * ((i - 1) % 32) + 16]
        xs.append((a[:, :128] + b[:, 128:256], a[:, 256:384] + b[:, 384:]))
    n = columns(xs, T, kr, ki, -1)
    parts = []
    for ri in range(2):
        for v in range(2):
            parts.append(jnp.stack([n[i][ri][8 * v:8 * v + 8] for i in range(32)], 0))
    return lane_swap(parts)

def stage_e(r5, T):
    x = jnp.concatenate([r5[q].reshape(256, 128).T for q in range(4)], 0).astype(bf16)
    o = mm(x, T["cs"][...])
    zs = []
    for v in range(8):
        b = 128 * (v // 2) + 32 * (v % 2)
        pr, pi = o[b:b + 32], o[b + 64:b + 96]
        re, im = pr[:, :256] - pi[:, 256:], pi[:, :256] + pr[:, 256:]
        if v:
            c, s = T["tw"][0, v:v + 1], T["tw"][1, v:v + 1]
            re, im = re * c - im * s, im * c + re * s
        zs.append((re, im))
    return fft_list(zs, 1)


NAMES = ("cs", "dfwd", "dinv", "row", "rowh", "ct", "cth", "tw", "twl", "t4", "ones", "spread", "pick")


def exact(x, table):
    hi = x.astype(bf16)
    rest = x - hi.astype(f32)
    mid = rest.astype(bf16)
    low = (rest - mid.astype(f32)).astype(bf16)
    return mm(hi, table) + mm(mid, table) + mm(low, table)


def body(field, target, *refs):
    n = len(NAMES)
    hbm, refs = dict(zip(NAMES, refs[:n])), refs[n:]
    r6, light_out = refs[:2]
    T, refs = dict(zip(NAMES, refs[2:2 + n])), refs[2 + n:]
    x1, r1, ts, tr, s2, r2, s3, r3, ls, lr, s4, r4, s5, r5, s6, kr, ki, tsem, ssem, rsem = refs
    row, col = lax.axis_index("rows"), lax.axis_index("cols")
    me = row * 8 + col

    def place(d):
        return (d // 8, lax.rem(d, 8))

    loads = [pltpu.make_async_copy(hbm[k], T[k], tsem.at[i]) for i, k in enumerate(NAMES)]
    barrier = pltpu.get_barrier_semaphore()

    for k in range(1, 8):
        pl.semaphore_signal(barrier, inc=1, device_id=(row, lax.rem(col + k, 8)), device_id_type=MESH)
    for k in range(1, 16):
        pl.semaphore_signal(barrier, inc=1, device_id=(lax.rem(row + k, 16), col), device_id_type=MESH)

    for copy in loads:
        copy.start()

    def copy_to(src, dst, slot, d):
        return pltpu.make_async_remote_copy(src, dst, ssem.at[slot], rsem.at[slot], device_id=d, device_id_type=MESH)

    def send_cols(src, dst, slot):
        for k in range(1, 8):
            d = lax.rem(col + k, 8)
            copy_to(src.at[d], dst.at[col], slot, (row, d)).start()
        if dst is r6:
            own = pltpu.make_async_copy(src.at[col], dst.at[col], tsem.at[0])
            own.start()
            own.wait()
        else:
            dst[pl.ds(col, 1)] = src[pl.ds(col, 1)]

    def send_all(src, dst, slot):
        def one(k, _):
            d = lax.rem(me + k, 128)
            copy_to(src.at[d], dst.at[me], slot, place(d)).start()
            return 0

        lax.fori_loop(1, 128, one, 0)
        dst[pl.ds(me, 1)] = src[pl.ds(me, 1)]

    def arrived(dst, slot):
        some = dst.at[pl.ds(0, dst.shape[0] - 1)]
        copy_to(some, some, slot, (row, col)).wait_recv()

    def sent(src, slot):
        some = src.at[pl.ds(0, src.shape[0] - 1)]
        copy_to(some, some, slot, (row, col)).wait_send()

    for c in range(8):
        x1[c] = field[:, 32 * c:32 * c + 32, :].astype(bf16)
    for copy in loads:
        copy.wait()
    lane = lax.broadcasted_iota(jnp.int32, (4, 16, 256), 2) % 16
    which = lax.broadcasted_iota(jnp.int32, (4, 16, 256), 1)
    rows = [jnp.broadcast_to(target[i, j:j + 1], (16, 256)) for i in range(2) for j in range(2)]
    chosen = jnp.where((lane == which).reshape(64, 256), jnp.concatenate(rows, 0), 0.0)
    goals = exact(chosen, T["spread"][...])
    for i in range(2):
        for g in range(4):
            ts[4 * i + g] = goals[32 * i:32 * i + 32, 128 * g:128 * g + 128]
    pl.semaphore_wait(barrier, 22)
    send_cols(x1, r1, 0)
    send_cols(ts, tr, 1)
    a, b = filt(me)
    kr[...] = a
    ki[...] = b
    arrived(r1, 0)
    for q, y in enumerate(stage_a(r1[...].astype(f32), T)):
        s2[32 * q:32 * q + 32] = y.astype(bf16)
    send_all(s2, r2, 2)
    arrived(r2, 2)
    for g, y in enumerate(stage_b(r2[...].astype(f32).reshape(32, 4, 8, 128), T, kr[...], ki[...])):
        for i in range(32):
            s3[4 * i + g] = y[i]
    send_all(s3, r3, 3)
    arrived(tr, 1)
    arrived(r3, 3)
    ys, light = stage_c(r3[...], tr[...].reshape(256, 128), T)
    for q, y in enumerate(ys):
        s4[32 * q:32 * q + 32] = y
    send_all(s4, r4, 4)
    ls[...] = light.reshape(8, 32, 128)
    send_cols(ls, lr, 5)
    arrived(r4, 4)
    for g, y in enumerate(stage_d(r4[...].reshape(32, 4, 16, 128), T, kr[...], ki[...])):
        for i in range(32):
            s5[4 * i + g] = y[i].astype(bf16)
    send_all(s5, r5, 6)
    arrived(lr, 5)
    parts = [jnp.concatenate([lr[4 * i + g] for g in range(4)], 1) for i in range(2)]
    picked = exact(jnp.concatenate(parts, 0), T["pick"][...]).reshape(4, 16, 256)
    light_out[...] = jnp.where(lane == which, picked, 0.0).sum(1)
    arrived(r5, 6)
    for c, (re, im) in enumerate(stage_e(r5[...].astype(f32).reshape(4, 32, 8, 128), T)):
        s6[c, 0] = re.astype(bf16)
        s6[c, 1] = im.astype(bf16)
    send_cols(s6, r6, 7)
    arrived(r6, 7)
    for slot, src in enumerate((x1, ts, s2, s3, s4, ls, s5, s6)):
        sent(src, slot)


def finish(r6, picked, grad, light):
    for c in range(8):
        grad[:, 32 * c:32 * c + 32, :] = r6[c].astype(f32)
    for i in range(2):
        light[i] = picked[2 * i:2 * i + 2]


def local(slm_field, target_light):
    T = tables()
    a = np.arange(256) // 16
    lanes = np.arange(512)
    view = 4 * (lanes // 128) + (lanes % 64) // 16
    spread = a[:, None] == view[None]
    T["spread"] = spread.astype(jnp.bfloat16)
    T["pick"] = (spread & (lanes % 128 % 16 == 0) & (lanes % 128 < 64)).T.astype(jnp.bfloat16)
    consts = [jnp.asarray(T[k]) for k in NAMES]
    vmem, anywhere = pl.BlockSpec(memory_space=pltpu.VMEM), pl.BlockSpec(memory_space=pl.ANY)
    V = pltpu.VMEM
    wide, f_all, b_all = V((8, 2, 32, 256), bf16), V((128, 8, 128), bf16), V((128, 16, 128), bf16)
    small = V((8, 32, 128), f32)
    blocks, picked = pl.pallas_call(
        body,
        out_shape=(jax.ShapeDtypeStruct((8, 2, 32, 256), bf16), jax.ShapeDtypeStruct((4, 256), f32)),
        in_specs=[vmem, vmem] + [anywhere] * len(NAMES),
        out_specs=(anywhere, vmem),
        scratch_shapes=[V(T[k].shape, T[k].dtype) for k in NAMES]
        + [wide, wide, small, small, f_all, f_all, b_all, b_all, small, small, b_all, b_all, f_all, f_all, wide]
        + [V((512, 128), f32)] * 2
        + [pltpu.SemaphoreType.DMA((len(NAMES),)), pltpu.SemaphoreType.DMA((8,)), pltpu.SemaphoreType.DMA((8,))],
        compiler_params=pltpu.CompilerParams(collective_id=0, has_side_effects=True, vmem_limit_bytes=56 << 20),
    )(slm_field, target_light, *consts)
    return pl.pallas_call(
        finish,
        out_shape=(jax.ShapeDtypeStruct((2, 256, 256), f32), jax.ShapeDtypeStruct((2, 2, 256), f32)),
        in_specs=[vmem, vmem],
        out_specs=(vmem, vmem),
    )(blocks, picked)


def solution(mesh):
    return jax.shard_map(
        local,
        mesh=mesh,
        in_specs=(P(None, "rows", "cols"), P("rows", "cols", None)),
        out_specs=(P(None, "rows", "cols"), P("rows", "cols", None)),
        check_vma=False,
    )
```

```python
import math

import jax
import jax.numpy as jnp
import numpy as np
from jax import lax
from jax.experimental import pallas as pl
from jax.experimental.pallas import tpu as pltpu
from jax.sharding import PartitionSpec as P

MESH = pl.DeviceIdType.MESH

f32, bf16 = jnp.float32, jnp.bfloat16

def mm(a, b, dims=((1,), (0,))):
    return lax.dot_general(a, b, (dims, ((), ())), preferred_element_type=f32)

def roll(x, shift):
    return pltpu.roll(x, shift, x.ndim - 1)

def turn(pair, angle):
    re, im = pair
    c, s = math.cos(angle), math.sin(angle)
    if abs(s) < 1e-9:
        return (re, im) if c > 0 else (-re, -im)
    if abs(c) < 1e-9:
        return (-im, re) if s > 0 else (im, -re)
    if abs(abs(c) - abs(s)) < 1e-9:
        k = abs(c)
        a, b = (re, im) if c > 0 else (-re, -im)
        if (s > 0) == (c > 0):
            return k * (a - b), k * (a + b)
        return k * (a + b), k * (b - a)
    return re * c - im * s, re * s + im * c

def fft_list(xs, sign):
    n = len(xs)
    if n == 1:
        return list(xs)
    even, odd = fft_list(xs[0::2], sign), fft_list(xs[1::2], sign)
    out = [None] * n
    for k in range(n // 2):
        t = turn(odd[k], sign * 2 * math.pi * k / n)
        e = even[k]
        out[k] = (e[0] + t[0], e[1] + t[1])
        out[k + n // 2] = (e[0] - t[0], e[1] - t[1])
    return out

def real_fft8(x):
    s = math.sqrt(0.5)
    a0, a1 = x[0] + x[4], x[0] - x[4]
    b0, b1 = x[2] + x[6], x[2] - x[6]
    c0, c1 = x[1] + x[5], x[1] - x[5]
    d0, d1 = x[3] + x[7], x[3] - x[7]
    e1, f1 = s * (c1 - d1), s * (c1 + d1)
    r1, r3 = a1 + e1, a1 - e1
    i1, i3 = -(b1 + f1), b1 - f1
    r2, i2 = a0 - b0, d0 - c0
    p, q = a0 + b0, c0 + d0
    return [(p + q, None), (r1, i1), (r2, i2), (r3, i3), (p - q, None), (r3, -i3), (r2, -i2), (r1, -i1)]

def lane_swap(xs):
    lane = lax.broadcasted_iota(jnp.int32, xs[0].shape, xs[0].ndim - 1)
    for step, (pairs, width) in enumerate((( ((0, 1), (2, 3)), 32), (((0, 2), (1, 3)), 64))):
        low = (lane // width) % 2 == 0
        out = [None] * 4
        for lo, hi in pairs:
            out[lo] = jnp.where(low, xs[lo], roll(xs[hi], width))
            out[hi] = jnp.where(low, roll(xs[lo], 128 - width), xs[hi])
        xs = out
    return xs

def by_i(x):
    lane = lax.broadcasted_iota(jnp.int32, x.shape, x.ndim - 1)
    return jnp.where(lane < 64, -1.0, 1.0) * roll(x, 64)

def tables():
    a = np.arange(256)
    t256 = 2 * np.pi * ((a[:, None] * a[None]) % 256) / 256
    C, S = np.cos(t256), np.sin(t256)
    cs = np.concatenate([C, S], 1)
    b = np.arange(128)
    t128 = 2 * np.pi * ((b[:, None] * b[None]) % 128) / 128
    c1, s1 = np.cos(t128), np.sin(t128)
    dfwd = np.block([[c1, -s1], [s1, c1]])
    dinv = np.block([[c1, s1], [-s1, c1]])
    taper = np.sin(np.pi * (a + 0.5) / 256) ** 2
    tr = taper[:, None] * C
    ti = -taper[:, None] * S
    rr, rim = tr / 256, ti / 256
    row = np.zeros((2, 256, 4, 2, 64))
    for g in range(4):
        s = slice(64 * g, 64 * g + 64)
        row[0, :, g, 0], row[0, :, g, 1] = rr[:, s], rim[:, s]
        row[1, :, g, 0], row[1, :, g, 1] = -rim[:, s], rr[:, s]
    row = row.reshape(512, 512)
    ct = np.concatenate([tr.T, ti.T], 1)
    cth = np.concatenate([tr, ti], 1)
    v0 = np.arange(8)
    th = 2 * np.pi * v0[:, None] * a[None] / 2048
    u0 = np.arange(32)
    t4 = 2 * np.pi * u0[:, None] * b[None] / 4096
    l = np.arange(128)
    ones = ((l[:, None] % 64) // 16 == (l[None] % 64) // 16) / 256.0
    B = lambda x: x.astype(jnp.bfloat16)
    F = lambda x: x.astype(np.float32)
    return dict(cs=B(cs), dfwd=B(dfwd), dinv=B(dinv), row=B(row), rowh=B(row.T.copy()), ct=B(ct), cth=B(cth),
                tw=F(np.stack([np.cos(th), np.sin(th)])),
                twl=F(np.broadcast_to(np.stack([np.cos(th), np.sin(th)])[..., None], (2, 8, 256, 128))),
                t4=F(np.stack([np.cos(t4), np.sin(t4)])), ones=B(ones))

def filt(me):
    q, k = me // 32, me % 32
    u0 = lax.broadcasted_iota(jnp.int32, (32, 16, 128), 0)
    w = lax.broadcasted_iota(jnp.int32, (32, 16, 128), 1)
    u1 = lax.broadcasted_iota(jnp.int32, (32, 16, 128), 2)
    u = 32 * u1 + u0
    v = 8 * (8 * k + w % 8) + 2 * q + w // 8
    fx = jnp.where(u < 2048, u, u - 4096).astype(f32) / 4096
    fy = jnp.where(v < 1024, v, v - 2048).astype(f32) / 2048
    s = fx * fx + fy * fy
    turns = 16000.0 * s / (jnp.sqrt(225.0 - s) + 15.0)
    quarters = 4.0 * (turns - jnp.floor(turns))
    nearest = jnp.floor(quarters + 0.5)
    z = (quarters - nearest) * (math.pi / 2)
    n = nearest.astype(jnp.int32)
    zz = z * z
    sine = z * (1 + zz * (-1 / 6 + zz * (1 / 120 + zz * (-1 / 5040 + zz / 362880))))
    cosine = 1 + zz * (-1 / 2 + zz * (1 / 24 + zz * (-1 / 720 + zz / 40320)))
    odd = n % 2 == 1
    c, d = jnp.where(odd, sine, cosine), jnp.where(odd, cosine, sine)
    half = 2.0 ** -23
    c = jnp.where((n % 4 == 1) | (n % 4 == 2), -half, half) * c
    d = jnp.where(n % 4 >= 2, half, -half) * d
    return c.reshape(512, 128), d.reshape(512, 128)

def turn_row(table, v):
    return table[0, v], table[1, v]


def columns(xs, T, kr, ki, sign):
    z = fft_list(xs, -1)
    lhs = []
    for u in range(32):
        c, s = T["t4"][0, u:u + 1], T["t4"][1, u:u + 1]
        re, im = z[u]
        lhs.append(jnp.concatenate([re * c + im * s, im * c - re * s], 1).astype(bf16))
    f = mm(jnp.concatenate(lhs, 0), T["dfwd"][...])
    fr, fi = f[:, :128], f[:, 128:]
    if sign > 0:
        pr, pi = fr * kr - fi * ki, fr * ki + fi * kr
    else:
        pr, pi = fr * kr + fi * ki, fi * kr - fr * ki
    g = mm(jnp.concatenate([pr, pi], 1).astype(bf16), T["dinv"][...])
    ys = []
    for u in range(32):
        c, s = T["t4"][0, u:u + 1], T["t4"][1, u:u + 1]
        re, im = g[16 * u:16 * u + 16, :128], g[16 * u:16 * u + 16, 128:]
        ys.append((re * c - im * s, im * c + re * s))
    return fft_list(ys, 1)


def halves(x, table):
    hi = x.astype(bf16)
    return mm(hi, table) + mm((x - hi.astype(f32)).astype(bf16), table)


NAMES = ("tw", "cs", "spread", "t4", "dfwd", "dinv", "row", "twl", "ct", "ones", "cth", "pick", "rowh")


def body(field, target, *refs):
    n = len(NAMES)
    hbm, refs = dict(zip(NAMES, refs[:n])), refs[n:]
    r6, light_out = refs[:2]
    T, refs = dict(zip(NAMES, refs[2:2 + n])), refs[2 + n:]
    (x0, tv, x1, r1, tr, goals, ra, s2, r2, xr, xi, nr, ni, s3, r3, ps, qs, nb, jb, sp, bk, hs, ls, lr, s4, r4, od, s5, r5,
     zr, zi, s6, kr, ki, tsem, ssem, rsem) = refs
    row, col = lax.axis_index("rows"), lax.axis_index("cols")
    z, high, low = 2 * (row & 1) + (col >> 2), row >> 1, col & 3
    me = 32 * z + 4 * high + low
    highs, lows = [(high + a) & 7 for a in range(8)], [(low + b) & 3 for b in range(4)]
    barrier = pltpu.get_barrier_semaphore()
    for k in range(1, 16):
        pl.semaphore_signal(barrier, inc=1, device_id=((row + k) & 15, col), device_id_type=MESH)
    for k in range(1, 8):
        pl.semaphore_signal(barrier, inc=1, device_id=(row, (col + k) & 7), device_id_type=MESH)
    first = [pltpu.make_async_copy(field, x0, tsem.at[n]), pltpu.make_async_copy(target, tv, tsem.at[n + 1])]
    loads = [pltpu.make_async_copy(hbm[k], T[k], tsem.at[i]) for i, k in enumerate(NAMES)]
    for copy in first + loads:
        copy.start()

    def need(*names):
        for k in names:
            loads[NAMES.index(k)].wait()

    def copy_to(src, dst, send, recv, d):
        return pltpu.make_async_remote_copy(src, dst, ssem.at[send], rsem.at[recv], device_id=d, device_id_type=MESH)

    def send_cols(src, dst, send, recv):
        for k in range(1, 8):
            d = (col + k) & 7
            copy_to(src(d), dst.at[col], send, recv, (row, d)).start()

    def send_group(src, dst, send, recv, j):
        q = ahead(j)
        up, left = q >> 1, 4 * (q & 1)
        for b in range(4):
            for a in range(8):
                if a or b or j:
                    d = 32 * q + 4 * highs[a] + lows[b]
                    copy_to(src(d, q, a, b), dst.at[me], send, recv + j, (2 * highs[a] + up, left + lows[b])).start()

    def arrived(dst, count, slot):
        some = dst.at[pl.ds(0, count)]
        copy_to(some, some, 0, slot, (row, col)).wait_recv()

    def sent(src, count, slot):
        some = src.at[pl.ds(0, count)]
        copy_to(some, some, slot, 0, (row, col)).wait_send()

    def ahead(j):
        return (z + j) & 3

    def behind(j):
        return (z + 4 - j) & 3

    for copy in first:
        copy.wait()
    for c in range(8):
        x1[c] = x0[:, 32 * c:32 * c + 32, :].astype(bf16)
    pl.semaphore_wait(barrier, 22)
    send_cols(lambda d: x1.at[d], r1, 0, 0)
    send_cols(lambda d: tv, tr, 1, 1)
    r1[pl.ds(col, 1)] = x1[pl.ds(col, 1)]
    tr[pl.ds(col, 1)] = tv[...][None]
    a, b = filt(me)
    kr[...] = a
    ki[...] = b

    need("tw", "cs")
    arrived(r1, 7, 0)
    zs = fft_list([(r1[c, 0].astype(f32), r1[c, 1].astype(f32)) for c in range(8)], -1)
    for v in range(8):
        q, w = v // 2, 32 * (v % 2)
        c, s = turn_row(T["tw"], v)
        re, im = zs[v]
        if v:
            re, im = re * c + im * s, im * c - re * s
        ra[q, w:w + 32] = jnp.concatenate([re, im], 1).astype(bf16)
        ra[q, 64 + w:96 + w] = jnp.concatenate([im, -re], 1).astype(bf16)
    for j in range(4):
        q = ahead(j)
        y = mm(T["cs"][...], ra[q], ((1,), (1,)))
        s2[pl.ds(32 * q, 32)] = y.reshape(32, 8, 128).astype(bf16)
        send_group(lambda d, *_: s2.at[d], r2, 2, 2, j)
        if j == 0:
            r2[pl.ds(me, 1)] = s2[pl.ds(me, 1)]

    need("spread")
    arrived(tr, 7, 1)
    lane = lax.broadcasted_iota(jnp.int32, (256, 256), 1) % 16
    which = lax.broadcasted_iota(jnp.int32, (256, 256), 0) % 16
    group = col & 3
    mine = [tr[c, pl.ds(col >> 2, 1)] for c in range(8)]
    rows = [jnp.broadcast_to(mine[j // 2][0, j % 2:j % 2 + 1], (16, 256)) for j in range(16)]
    goals[...] = halves(jnp.where(lane == which, jnp.concatenate(rows, 0), 0.0), T["spread"][group])

    need("t4", "dfwd", "dinv")
    for j in range(4):
        q = behind(j)
        arrived(r2, 32 if j else 31, 2 + j)
        x = r2[pl.ds(32 * q, 32)].astype(f32).reshape(8, 4, 8, 128)
        b = lane_swap([x[:, g] for g in range(4)])
        for v in range(2):
            xr[q, :, 8 * v:8 * v + 8] = b[v]
            xi[q, :, 8 * v:8 * v + 8] = b[2 + v]
    xs = [(xr[i % 4, i // 4], xi[i % 4, i // 4]) for i in range(32)]
    for i, (re, im) in enumerate(columns(xs, T, kr[...], ki[...], 1)):
        k = (i - 1) % 32
        for x, part in ((nr, re.astype(bf16)), (ni, im.astype(bf16))):
            x[0, i % 4, i // 4] = part
            x[1, k % 4, k // 4] = part
    need("row")
    for j in range(4):
        q = ahead(j)
        parts = [x[d, q].reshape(128, 128) for x in (nr, ni) for d in range(2)]
        o = mm(jnp.concatenate(parts, 1), T["row"][...])
        for g in range(4):
            s3[pl.ds(8 * q, 8), g] = o[:, 128 * g:128 * g + 128].reshape(8, 16, 128).astype(bf16)
        send_group(lambda d, q, a, b: s3.at[8 * q + highs[a], lows[b]], r3, 3, 6, j)
        if j == 0:
            r3[pl.ds(me, 1)] = s3[8 * z + high, pl.ds(low, 1)]

    need("twl", "ct", "ones", "cth", "pick", "rowh")
    for j in range(4):
        q = behind(j)
        arrived(r3, 32 if j else 31, 6 + j)
        x = r3[pl.ds(32 * q, 32)].astype(f32).reshape(32, 2, 8, 128)
        cols = []
        for v in range(2):
            xv = x[:, v].reshape(256, 128)
            cols.append(jnp.concatenate([xv.astype(bf16), by_i(xv).astype(bf16)], 0))
        o = mm(T["cs"][...], jnp.concatenate(cols, 1))
        for v in range(2):
            zv = o[:, 128 * v:128 * v + 128]
            ps[2 * q + v] = zv * T["twl"][0, 2 * q + v]
            qs[2 * q + v] = zv * T["twl"][1, 2 * q + v]
    for m in range(0, 256, 32):
        part = slice(m, m + 32)
        for c, (p, q) in enumerate(fft_list([(ps[v, part], qs[v, part]) for v in range(8)], 1)):
            near = p + by_i(q)
            nb[c, part] = near.astype(bf16)
            jb[c, part] = by_i(near).astype(bf16)
    sums = []
    for c in range(8):
        d = (c + 1) % 8
        even = jnp.concatenate([nb[c], jb[c]], 0)
        odd = jnp.concatenate([nb[c, 128:], nb[d, :128], jb[c, 128:], jb[d, :128]], 0)
        o = mm(T["ct"][...], jnp.concatenate([even, odd], 1))
        for j in range(2):
            s = o[:, 128 * j:128 * j + 128]
            sp[2 * c + j] = s
            sums.append((s * s).reshape(16, 16, 128).sum(1))
    light = halves(jnp.concatenate(sums, 0), T["ones"][...])
    wt = 4.0 * (light - goals[...])
    for c in range(8):
        cols = []
        for j in (2 * c, 2 * c + 1):
            w = sp[j] * jnp.concatenate([jnp.broadcast_to(wt[r:r + 1], (16, 128)) for r in range(16 * j, 16 * j + 16)], 0)
            cols.append(jnp.concatenate([w.astype(bf16), (-by_i(w)).astype(bf16)], 0))
        o = mm(T["cth"][...], jnp.concatenate(cols, 1))
        bk[2 * c] = o[:, :128]
        bk[2 * c + 1] = o[:, 128:]
    for m in range(0, 256, 32):
        part = slice(m, m + 32)
        xs = []
        for c in range(8):
            if m < 128:
                xs.append(bk[2 * c, part] + bk[(2 * c - 1) % 16, m + 128:m + 160])
            else:
                xs.append(bk[2 * c + 1, m - 128:m - 96] + bk[2 * c, part])
        for v, (e, f) in enumerate(real_fft8(xs)):
            c, s = T["twl"][0, v, part], T["twl"][1, v, part]
            if f is None:
                p, q = e * c, -e * s
            else:
                p, q = e * c + f * s, f * c - e * s
            h = p + by_i(q)
            w = slice(128 * (v % 2), 128 * (v % 2) + 128)
            hs[v // 2, part, w] = h.astype(bf16)
            hs[v // 2, 256 + m:288 + m, w] = (-by_i(h)).astype(bf16)
    for j in range(4):
        q = ahead(j)
        y = mm(T["cs"][...], hs[q])
        pair = [y[:, 128 * v:128 * v + 128].reshape(32, 1, 8, 128) for v in range(2)]
        s4[pl.ds(32 * q, 32)] = jnp.concatenate(pair, 1).reshape(32, 16, 128).astype(bf16)
        send_group(lambda d, *_: s4.at[d], r4, 4, 10, j)
        if j == 0:
            r4[pl.ds(me, 1)] = s4[pl.ds(me, 1)]
    views = jnp.where(lane == which, halves(light, T["pick"][group]), 0.0).reshape(16, 16, 256).sum(1)
    for c in range(8):
        ls[c] = views[2 * c:2 * c + 2]
    send_cols(lambda d: ls.at[d], lr, 5, 14)
    lr[pl.ds(col, 1)] = ls[pl.ds(col, 1)]

    for j in range(4):
        q = behind(j)
        arrived(r4, 32 if j else 31, 10 + j)
        x = r4[pl.ds(32 * q, 32)].reshape(8, 4, 16, 128)
        o = mm(jnp.concatenate([x[:, g].reshape(128, 128) for g in range(4)], 1), T["rowh"][...])
        od[q] = o.reshape(8, 16, 512)
    xs = []
    for i in range(32):
        a, b, k = i % 4, i // 4, (i - 1) % 32
        c, d = k % 4, k // 4
        xs.append((od[a, b, :, :128] + od[c, d, :, 128:256], od[a, b, :, 256:384] + od[c, d, :, 384:]))
    for i, (re, im) in enumerate(columns(xs, T, kr[...], ki[...], -1)):
        xr[i % 4, i // 4] = re
        xi[i % 4, i // 4] = im
    for j in range(4):
        q = ahead(j)
        parts = lane_swap([x[q, :, 8 * v:8 * v + 8] for x in (xr, xi) for v in range(2)])
        for g in range(4):
            s5[pl.ds(8 * q, 8), g] = parts[g].astype(bf16)
        send_group(lambda d, q, a, b: s5.at[8 * q + highs[a], lows[b]], r5, 6, 15, j)
        if j == 0:
            r5[pl.ds(me, 1)] = s5[8 * z + high, pl.ds(low, 1)]
    arrived(lr, 7, 14)
    for i in range(2):
        light_out[2 * i:2 * i + 2] = (lr[4 * i] + lr[4 * i + 1]) + (lr[4 * i + 2] + lr[4 * i + 3])

    for j in range(4):
        q = behind(j)
        arrived(r5, 32 if j else 31, 15 + j)
        x = r5[pl.ds(32 * q, 32)].astype(f32).reshape(256, 128).T.astype(bf16)
        o = mm(x, T["cs"][...])
        for v in range(2):
            pr, pi = o[32 * v:32 * v + 32], o[64 + 32 * v:96 + 32 * v]
            re, im = pr[:, :256] - pi[:, 256:], pi[:, :256] + pr[:, 256:]
            c, s = turn_row(T["tw"], 2 * q + v)
            zr[2 * q + v] = re * c - im * s
            zi[2 * q + v] = im * c + re * s
    for c, (re, im) in enumerate(fft_list([(zr[v], zi[v]) for v in range(8)], 1)):
        s6[c, 0] = re.astype(bf16)
        s6[c, 1] = im.astype(bf16)
    send_cols(lambda d: s6.at[d], r6, 7, 19)
    own = pltpu.make_async_copy(s6.at[col], r6.at[col], tsem.at[0])
    own.start()
    for slot, (src, count) in enumerate(((x1, 7), (tr, 7), (r2, 127), (r3, 127), (r4, 127), (ls, 7), (r5, 127), (s6, 7))):
        sent(src, count, slot)
    own.wait()
    arrived(r6, 7, 19)


def finish(blocks, picked, grad, light):
    for c in range(8):
        grad[:, 32 * c:32 * c + 32, :] = blocks[c].astype(f32)
    for i in range(2):
        light[i] = picked[2 * i:2 * i + 2]


def local(slm_field, target_light):
    T = tables()
    T["tw"] = T["tw"].reshape(2, 8, 1, 256)
    view, lane = np.arange(256) // 16, np.arange(128)
    spread = np.stack([view[:, None] == 4 * g + (lane % 64) // 16 for g in range(4)])
    T["spread"] = spread.astype(jnp.bfloat16)
    T["pick"] = (spread & (lane % 16 == 0) & (lane < 64)).transpose(0, 2, 1).astype(jnp.bfloat16)
    consts = [jnp.asarray(T[k]) for k in NAMES]
    vmem, anywhere = pl.BlockSpec(memory_space=pltpu.VMEM), pl.BlockSpec(memory_space=pl.ANY)
    V = pltpu.VMEM
    block, f_all, b_all = V((8, 2, 32, 256), bf16), V((128, 8, 128), bf16), V((128, 16, 128), bf16)
    line, lines = V((8, 256, 128), bf16), V((8, 256, 128), f32)
    scratch = dict(
        x0=V((2, 256, 256), f32), tv=V((2, 2, 256), f32), x1=block, r1=block, tr=V((8, 2, 2, 256), f32), goals=V((256, 128), f32),
        ra=V((4, 128, 512), bf16), s2=f_all, r2=f_all, xr=V((4, 8, 16, 128), f32), xi=V((4, 8, 16, 128), f32),
        nr=V((2, 4, 8, 16, 128), bf16), ni=V((2, 4, 8, 16, 128), bf16), s3=V((32, 4, 16, 128), bf16), r3=b_all, ps=lines, qs=lines,
        nb=line, jb=line, sp=V((16, 256, 128), f32), bk=V((16, 256, 128), f32), hs=V((4, 512, 256), bf16),
        ls=V((8, 2, 256), f32), lr=V((8, 2, 256), f32), s4=b_all, r4=b_all, od=V((4, 8, 16, 512), f32),
        s5=V((32, 4, 8, 128), bf16), r5=f_all, zr=V((8, 32, 256), f32), zi=V((8, 32, 256), f32), s6=block,
        kr=V((512, 128), f32), ki=V((512, 128), f32),
    )
    blocks, picked = pl.pallas_call(
        body,
        out_shape=(jax.ShapeDtypeStruct((8, 2, 32, 256), bf16), jax.ShapeDtypeStruct((4, 256), f32)),
        in_specs=[anywhere] * (2 + len(NAMES)),
        out_specs=(anywhere, vmem),
        scratch_shapes=[V(T[k].shape, T[k].dtype) for k in NAMES]
        + list(scratch.values())
        + [pltpu.SemaphoreType.DMA((len(NAMES) + 2,)), pltpu.SemaphoreType.DMA((8,)), pltpu.SemaphoreType.DMA((20,))],
        compiler_params=pltpu.CompilerParams(collective_id=0, has_side_effects=True, vmem_limit_bytes=60 << 20),
    )(slm_field, target_light, *consts)
    return pl.pallas_call(
        finish,
        out_shape=(jax.ShapeDtypeStruct((2, 256, 256), f32), jax.ShapeDtypeStruct((2, 2, 256), f32)),
        in_specs=[vmem, vmem],
        out_specs=(vmem, vmem),
    )(blocks, picked)


def solution(mesh):
    return jax.shard_map(
        local,
        mesh=mesh,
        in_specs=(P(None, "rows", "cols"), P("rows", "cols", None)),
        out_specs=(P(None, "rows", "cols"), P("rows", "cols", None)),
        check_vma=False,
    )
```

```python
import math

import jax
import jax.numpy as jnp
import numpy as np
from jax import lax
from jax.experimental import pallas as pl
from jax.experimental.pallas import tpu as pltpu
from jax.sharding import PartitionSpec as P

MESH = pl.DeviceIdType.MESH

f32, bf16 = jnp.float32, jnp.bfloat16

def mm(a, b, dims=((1,), (0,))):
    return lax.dot_general(a, b, (dims, ((), ())), preferred_element_type=f32)

def roll(x, shift):
    return pltpu.roll(x, shift, x.ndim - 1)

def turn(pair, angle):
    re, im = pair
    c, s = math.cos(angle), math.sin(angle)
    if abs(s) < 1e-9:
        return (re, im) if c > 0 else (-re, -im)
    if abs(c) < 1e-9:
        return (-im, re) if s > 0 else (im, -re)
    if abs(abs(c) - abs(s)) < 1e-9:
        k = abs(c)
        a, b = (re, im) if c > 0 else (-re, -im)
        if (s > 0) == (c > 0):
            return k * (a - b), k * (a + b)
        return k * (a + b), k * (b - a)
    return re * c - im * s, re * s + im * c

def fft_list(xs, sign):
    n = len(xs)
    if n == 1:
        return list(xs)
    even, odd = fft_list(xs[0::2], sign), fft_list(xs[1::2], sign)
    out = [None] * n
    for k in range(n // 2):
        t = turn(odd[k], sign * 2 * math.pi * k / n)
        e = even[k]
        out[k] = (e[0] + t[0], e[1] + t[1])
        out[k + n // 2] = (e[0] - t[0], e[1] - t[1])
    return out

def real_fft8(x):
    s = math.sqrt(0.5)
    a0, a1 = x[0] + x[4], x[0] - x[4]
    b0, b1 = x[2] + x[6], x[2] - x[6]
    c0, c1 = x[1] + x[5], x[1] - x[5]
    d0, d1 = x[3] + x[7], x[3] - x[7]
    e1, f1 = s * (c1 - d1), s * (c1 + d1)
    r1, r3 = a1 + e1, a1 - e1
    i1, i3 = -(b1 + f1), b1 - f1
    r2, i2 = a0 - b0, d0 - c0
    p, q = a0 + b0, c0 + d0
    return [(p + q, None), (r1, i1), (r2, i2), (r3, i3), (p - q, None), (r3, -i3), (r2, -i2), (r1, -i1)]

def lane_swap(xs):
    lane = lax.broadcasted_iota(jnp.int32, xs[0].shape, xs[0].ndim - 1)
    for step, (pairs, width) in enumerate((( ((0, 1), (2, 3)), 32), (((0, 2), (1, 3)), 64))):
        low = (lane // width) % 2 == 0
        out = [None] * 4
        for lo, hi in pairs:
            out[lo] = jnp.where(low, xs[lo], roll(xs[hi], width))
            out[hi] = jnp.where(low, roll(xs[lo], 128 - width), xs[hi])
        xs = out
    return xs

def by_i(x):
    lane = lax.broadcasted_iota(jnp.int32, x.shape, x.ndim - 1)
    return jnp.where(lane < 64, -1.0, 1.0) * roll(x, 64)

def tables():
    a = np.arange(256)
    t256 = 2 * np.pi * ((a[:, None] * a[None]) % 256) / 256
    C, S = np.cos(t256), np.sin(t256)
    cs = np.concatenate([C, S], 1)
    b = np.arange(128)
    t128 = 2 * np.pi * ((b[:, None] * b[None]) % 128) / 128
    c1, s1 = np.cos(t128), np.sin(t128)
    dfwd = np.block([[c1, -s1], [s1, c1]])
    dinv = np.block([[c1, s1], [-s1, c1]])
    taper = np.sin(np.pi * (a + 0.5) / 256) ** 2
    tr = taper[:, None] * C
    ti = -taper[:, None] * S
    rr, rim = tr / 256, ti / 256
    row = np.zeros((2, 256, 4, 2, 64))
    for g in range(4):
        s = slice(64 * g, 64 * g + 64)
        row[0, :, g, 0], row[0, :, g, 1] = rr[:, s], rim[:, s]
        row[1, :, g, 0], row[1, :, g, 1] = -rim[:, s], rr[:, s]
    row = row.reshape(512, 512)
    ct = np.concatenate([tr.T, ti.T], 1)
    cth = np.concatenate([tr, ti], 1)
    v0 = np.arange(8)
    th = 2 * np.pi * v0[:, None] * a[None] / 2048
    u0 = np.arange(32)
    t4 = 2 * np.pi * u0[:, None] * b[None] / 4096
    l = np.arange(128)
    ones = ((l[:, None] % 64) // 16 == (l[None] % 64) // 16) / 256.0
    B = lambda x: x.astype(jnp.bfloat16)
    F = lambda x: x.astype(np.float32)
    return dict(cs=B(cs), dfwd=B(dfwd), dinv=B(dinv), row=B(row), rowh=B(row.T.copy()), ct=B(ct), cth=B(cth),
                tw=F(np.stack([np.cos(th), np.sin(th)])),
                twl=F(np.broadcast_to(np.stack([np.cos(th), np.sin(th)])[..., None], (2, 8, 256, 128))),
                t4=F(np.stack([np.cos(t4), np.sin(t4)])), ones=B(ones))

def filt(me):
    q, k = me // 32, me % 32
    u0 = lax.broadcasted_iota(jnp.int32, (32, 16, 128), 0)
    w = lax.broadcasted_iota(jnp.int32, (32, 16, 128), 1)
    u1 = lax.broadcasted_iota(jnp.int32, (32, 16, 128), 2)
    u = 32 * u1 + u0
    v = 8 * (8 * k + w % 8) + 2 * q + w // 8
    fx = jnp.where(u < 2048, u, u - 4096).astype(f32) / 4096
    fy = jnp.where(v < 1024, v, v - 2048).astype(f32) / 2048
    s = fx * fx + fy * fy
    turns = 16000.0 * s / (jnp.sqrt(225.0 - s) + 15.0)
    quarters = 4.0 * (turns - jnp.floor(turns))
    nearest = jnp.floor(quarters + 0.5)
    z = (quarters - nearest) * (math.pi / 2)
    n = nearest.astype(jnp.int32)
    zz = z * z
    sine = z * (1 + zz * (-1 / 6 + zz * (1 / 120 + zz * (-1 / 5040 + zz / 362880))))
    cosine = 1 + zz * (-1 / 2 + zz * (1 / 24 + zz * (-1 / 720 + zz / 40320)))
    odd = n % 2 == 1
    c, d = jnp.where(odd, sine, cosine), jnp.where(odd, cosine, sine)
    half = 2.0 ** -23
    c = jnp.where((n % 4 == 1) | (n % 4 == 2), -half, half) * c
    d = jnp.where(n % 4 >= 2, half, -half) * d
    return c.reshape(512, 128), d.reshape(512, 128)

FAR_FIRST = sorted(
    ((a, b) for a in range(8) for b in range(4)),
    key=lambda p: -(min(p[0] >> 1, 4 - (p[0] >> 1)) + 2 * (p[0] & 1) + min(p[1], 4 - p[1])),
)
QUARTERS = (2, 3, 1, 0)
STEP = 8


def turn_row(table, v):
    return table[0, v], table[1, v]


def columns(xs, T, kr, ki, sign):
    z = fft_list(xs, -1)
    lhs = []
    for u in range(32):
        c, s = T["t4"][0, u:u + 1], T["t4"][1, u:u + 1]
        re, im = z[u]
        lhs.append(jnp.concatenate([re * c + im * s, im * c - re * s], 1).astype(bf16))
    f = mm(jnp.concatenate(lhs, 0), T["dfwd"][...])
    fr, fi = f[:, :128], f[:, 128:]
    if sign > 0:
        pr, pi = fr * kr - fi * ki, fr * ki + fi * kr
    else:
        pr, pi = fr * kr + fi * ki, fi * kr - fr * ki
    g = mm(jnp.concatenate([pr, pi], 1).astype(bf16), T["dinv"][...])
    ys = []
    for u in range(32):
        c, s = T["t4"][0, u:u + 1], T["t4"][1, u:u + 1]
        re, im = g[16 * u:16 * u + 16, :128], g[16 * u:16 * u + 16, 128:]
        ys.append((re * c - im * s, im * c + re * s))
    return fft_list(ys, 1)


def halves(x, table):
    hi = x.astype(bf16)
    return mm(hi, table) + mm((x - hi.astype(f32)).astype(bf16), table)


NAMES = ("tw", "cs", "spread", "t4", "dfwd", "dinv", "row", "twl", "ct", "ones", "cth", "pick", "rowh")


def body(field, target, *refs):
    n = len(NAMES)
    hbm, refs = dict(zip(NAMES, refs[:n])), refs[n:]
    r6, light_out = refs[:2]
    T, refs = dict(zip(NAMES, refs[2:2 + n])), refs[2 + n:]
    (x0, tv, x1, r1, tr, goals, ra, s2, r2, xr, xi, nr, ni, s3, r3, ps, qs, nb, jb, sp, bk, hs, ls, lr, s4, r4, od, s5, r5,
     zr, zi, s6, kr, ki, tsem, ssem, rsem) = refs
    row, col = lax.axis_index("rows"), lax.axis_index("cols")
    z, high, low = 2 * (row & 1) + (col >> 2), row >> 1, col & 3
    me = 32 * z + 4 * high + low
    highs = [((high + (a & 6)) & 6) + ((high + a) & 1) for a in range(8)]
    lows = [(low + b) & 3 for b in range(4)]
    barrier = pltpu.get_barrier_semaphore()
    for k in range(1, 16):
        pl.semaphore_signal(barrier, inc=1, device_id=((row + k) & 15, col), device_id_type=MESH)
    for k in range(1, 8):
        pl.semaphore_signal(barrier, inc=1, device_id=(row, (col + k) & 7), device_id_type=MESH)
    first = [pltpu.make_async_copy(field, x0, tsem.at[n]), pltpu.make_async_copy(target, tv, tsem.at[n + 1])]
    loads = [pltpu.make_async_copy(hbm[k], T[k], tsem.at[i]) for i, k in enumerate(NAMES)]
    for copy in first + loads:
        copy.start()

    def need(*names):
        for k in names:
            loads[NAMES.index(k)].wait()

    def copy_to(src, dst, send, recv, d):
        return pltpu.make_async_remote_copy(src, dst, ssem.at[send], rsem.at[recv], device_id=d, device_id_type=MESH)

    def send_cols(src, dst, send, recv):
        for k in (4, 1, 5, 3, 6, 2, 7):
            d = ((col ^ k) & 4) + ((col + k) & 3)
            copy_to(src(d), dst.at[col], send, recv, (row, d)).start()

    def send_group(src, dst, send, recv, j):
        q = ahead(j)
        up, left = q >> 1, 4 * (q & 1)
        for a, b in FAR_FIRST:
            if a or b or QUARTERS[j]:
                d = 32 * q + 4 * highs[a] + lows[b]
                copy_to(src(d, q, a, b), dst.at[me], send, recv + j, (2 * highs[a] + up, left + lows[b])).start()

    def arrived(dst, count, slot):
        some = dst.at[pl.ds(0, count)]
        copy_to(some, some, 0, slot, (row, col)).wait_recv()

    def sent(src, count, slot):
        some = src.at[pl.ds(0, count)]
        copy_to(some, some, slot, 0, (row, col)).wait_send()

    def ahead(j):
        return z ^ QUARTERS[j]

    def behind(j):
        return z ^ QUARTERS[j]

    for copy in first:
        copy.wait()
    for c in range(8):
        x1[c] = x0[:, 32 * c:32 * c + 32, :].astype(bf16)
    pl.semaphore_wait(barrier, 22)
    send_cols(lambda d: x1.at[d], r1, 0, 0)
    send_cols(lambda d: tv, tr, 1, 1)
    r1[pl.ds(col, 1)] = x1[pl.ds(col, 1)]
    tr[pl.ds(col, 1)] = tv[...][None]
    a, b = filt(me)
    kr[...] = a
    ki[...] = b

    need("tw", "cs")
    arrived(r1, 7, 0)
    zs = fft_list([(r1[c, 0].astype(f32), r1[c, 1].astype(f32)) for c in range(8)], -1)
    for v in range(8):
        q, w = v // 2, 32 * (v % 2)
        c, s = turn_row(T["tw"], v)
        re, im = zs[v]
        if v:
            re, im = re * c + im * s, im * c - re * s
        ra[q, w:w + 32] = jnp.concatenate([re, im], 1).astype(bf16)
        ra[q, 64 + w:96 + w] = jnp.concatenate([im, -re], 1).astype(bf16)
    for j in range(4):
        q = ahead(j)
        y = mm(T["cs"][...], ra[q], ((1,), (1,)))
        s2[pl.ds(32 * q, 32)] = y.reshape(32, 8, 128).astype(bf16)
        send_group(lambda d, *_: s2.at[d], r2, 2, 2, j)
        if QUARTERS[j] == 0:
            r2[pl.ds(me, 1)] = s2[pl.ds(me, 1)]

    need("spread")
    arrived(tr, 7, 1)
    lane = lax.broadcasted_iota(jnp.int32, (256, 256), 1) % 16
    which = lax.broadcasted_iota(jnp.int32, (256, 256), 0) % 16
    group = col & 3
    mine = [tr[c, pl.ds(col >> 2, 1)] for c in range(8)]
    rows = [jnp.broadcast_to(mine[j // 2][0, j % 2:j % 2 + 1], (16, 256)) for j in range(16)]
    goals[...] = halves(jnp.where(lane == which, jnp.concatenate(rows, 0), 0.0), T["spread"][group])

    need("t4", "dfwd", "dinv")
    for j in range(4):
        q = behind(j)
        arrived(r2, 32 if QUARTERS[j] else 31, 2 + j)
        x = r2[pl.ds(32 * q, 32)].astype(f32).reshape(8, 4, 8, 128)
        b = lane_swap([x[:, g] for g in range(4)])
        for v in range(2):
            xr[q, :, 8 * v:8 * v + 8] = b[v]
            xi[q, :, 8 * v:8 * v + 8] = b[2 + v]
    xs = [(xr[i % 4, i // 4], xi[i % 4, i // 4]) for i in range(32)]
    for i, (re, im) in enumerate(columns(xs, T, kr[...], ki[...], 1)):
        k = (i - 1) % 32
        for x, part in ((nr, re.astype(bf16)), (ni, im.astype(bf16))):
            x[0, i % 4, i // 4] = part
            x[1, k % 4, k // 4] = part
    need("row")
    for j in range(4):
        q = ahead(j)
        parts = [x[d, q].reshape(128, 128) for x in (nr, ni) for d in range(2)]
        o = mm(jnp.concatenate(parts, 1), T["row"][...])
        for g in range(4):
            s3[pl.ds(8 * q, 8), g] = o[:, 128 * g:128 * g + 128].reshape(8, 16, 128).astype(bf16)
        send_group(lambda d, q, a, b: s3.at[8 * q + highs[a], lows[b]], r3, 3, 6, j)
        if QUARTERS[j] == 0:
            r3[pl.ds(me, 1)] = s3[8 * z + high, pl.ds(low, 1)]

    need("twl", "ct", "ones", "cth", "pick", "rowh")
    for j in range(4):
        q = behind(j)
        arrived(r3, 32 if QUARTERS[j] else 31, 6 + j)
        x = r3[pl.ds(32 * q, 32)].astype(f32).reshape(32, 2, 8, 128)
        cols = []
        for v in range(2):
            xv = x[:, v].reshape(256, 128)
            cols.append(jnp.concatenate([xv.astype(bf16), by_i(xv).astype(bf16)], 0))
        o = mm(T["cs"][...], jnp.concatenate(cols, 1))
        for v in range(2):
            zv = o[:, 128 * v:128 * v + 128]
            ps[2 * q + v] = zv * T["twl"][0, 2 * q + v]
            qs[2 * q + v] = zv * T["twl"][1, 2 * q + v]
    for m in range(0, 256, 32):
        part = slice(m, m + 32)
        for c, (p, q) in enumerate(fft_list([(ps[v, part], qs[v, part]) for v in range(8)], 1)):
            near = p + by_i(q)
            nb[c, part] = near.astype(bf16)
            jb[c, part] = by_i(near).astype(bf16)
    lights = []
    for first in range(0, 8, STEP):
        sums = []
        for c in range(first, first + STEP):
            d = (c + 1) % 8
            even = jnp.concatenate([nb[c], jb[c]], 0)
            odd = jnp.concatenate([nb[c, 128:], nb[d, :128], jb[c, 128:], jb[d, :128]], 0)
            o = mm(T["ct"][...], jnp.concatenate([even, odd], 1))
            for j in range(2):
                s = o[:, 128 * j:128 * j + 128]
                sp[2 * c + j] = s
                sums.append((s * s).reshape(16, 16, 128).sum(1))
        light = halves(jnp.concatenate(sums, 0), T["ones"][...])
        wt = 4.0 * (light - goals[32 * first:32 * first + 32 * STEP])
        lights.append(light)
        for c in range(first, first + STEP):
            cols = []
            for j in (2 * c, 2 * c + 1):
                rows = range(16 * j - 32 * first, 16 * j - 32 * first + 16)
                w = sp[j] * jnp.concatenate([jnp.broadcast_to(wt[r:r + 1], (16, 128)) for r in rows], 0)
                cols.append(jnp.concatenate([w.astype(bf16), (-by_i(w)).astype(bf16)], 0))
            o = mm(T["cth"][...], jnp.concatenate(cols, 1))
            bk[2 * c] = o[:, :128]
            bk[2 * c + 1] = o[:, 128:]
    light = jnp.concatenate(lights, 0)
    for m in range(0, 256, 32):
        part = slice(m, m + 32)
        xs = []
        for c in range(8):
            if m < 128:
                xs.append(bk[2 * c, part] + bk[(2 * c - 1) % 16, m + 128:m + 160])
            else:
                xs.append(bk[2 * c + 1, m - 128:m - 96] + bk[2 * c, part])
        for v, (e, f) in enumerate(real_fft8(xs)):
            c, s = T["twl"][0, v, part], T["twl"][1, v, part]
            if f is None:
                p, q = e * c, -e * s
            else:
                p, q = e * c + f * s, f * c - e * s
            h = p + by_i(q)
            w = slice(128 * (v % 2), 128 * (v % 2) + 128)
            hs[v // 2, part, w] = h.astype(bf16)
            hs[v // 2, 256 + m:288 + m, w] = (-by_i(h)).astype(bf16)
    for j in range(4):
        q = ahead(j)
        y = mm(T["cs"][...], hs[q])
        pair = [y[:, 128 * v:128 * v + 128].reshape(32, 1, 8, 128) for v in range(2)]
        s4[pl.ds(32 * q, 32)] = jnp.concatenate(pair, 1).reshape(32, 16, 128).astype(bf16)
        send_group(lambda d, *_: s4.at[d], r4, 4, 10, j)
        if QUARTERS[j] == 0:
            r4[pl.ds(me, 1)] = s4[pl.ds(me, 1)]
    views = jnp.where(lane == which, halves(light, T["pick"][group]), 0.0).reshape(16, 16, 256).sum(1)
    for c in range(8):
        ls[c] = views[2 * c:2 * c + 2]
    send_cols(lambda d: ls.at[d], lr, 5, 14)
    lr[pl.ds(col, 1)] = ls[pl.ds(col, 1)]

    for j in range(4):
        q = behind(j)
        arrived(r4, 32 if QUARTERS[j] else 31, 10 + j)
        x = r4[pl.ds(32 * q, 32)].reshape(8, 4, 16, 128)
        o = mm(jnp.concatenate([x[:, g].reshape(128, 128) for g in range(4)], 1), T["rowh"][...])
        od[q] = o.reshape(8, 16, 512)
    xs = []
    for i in range(32):
        a, b, k = i % 4, i // 4, (i - 1) % 32
        c, d = k % 4, k // 4
        xs.append((od[a, b, :, :128] + od[c, d, :, 128:256], od[a, b, :, 256:384] + od[c, d, :, 384:]))
    for i, (re, im) in enumerate(columns(xs, T, kr[...], ki[...], -1)):
        xr[i % 4, i // 4] = re
        xi[i % 4, i // 4] = im
    for j in range(4):
        q = ahead(j)
        parts = lane_swap([x[q, :, 8 * v:8 * v + 8] for x in (xr, xi) for v in range(2)])
        for g in range(4):
            s5[pl.ds(8 * q, 8), g] = parts[g].astype(bf16)
        send_group(lambda d, q, a, b: s5.at[8 * q + highs[a], lows[b]], r5, 6, 15, j)
        if QUARTERS[j] == 0:
            r5[pl.ds(me, 1)] = s5[8 * z + high, pl.ds(low, 1)]
    arrived(lr, 7, 14)
    for i in range(2):
        light_out[2 * i:2 * i + 2] = (lr[4 * i] + lr[4 * i + 1]) + (lr[4 * i + 2] + lr[4 * i + 3])

    for j in range(4):
        q = behind(j)
        arrived(r5, 32 if QUARTERS[j] else 31, 15 + j)
        x = r5[pl.ds(32 * q, 32)].astype(f32).reshape(256, 128).T.astype(bf16)
        o = mm(x, T["cs"][...])
        for v in range(2):
            pr, pi = o[32 * v:32 * v + 32], o[64 + 32 * v:96 + 32 * v]
            re, im = pr[:, :256] - pi[:, 256:], pi[:, :256] + pr[:, 256:]
            c, s = turn_row(T["tw"], 2 * q + v)
            zr[2 * q + v] = re * c - im * s
            zi[2 * q + v] = im * c + re * s
    for c, (re, im) in enumerate(fft_list([(zr[v], zi[v]) for v in range(8)], 1)):
        s6[c, 0] = re.astype(bf16)
        s6[c, 1] = im.astype(bf16)
    send_cols(lambda d: s6.at[d], r6, 7, 19)
    own = pltpu.make_async_copy(s6.at[col], r6.at[col], tsem.at[0])
    own.start()
    for slot, (src, count) in enumerate(((x1, 7), (tr, 7), (r2, 127), (r3, 127), (r4, 127), (ls, 7), (r5, 127), (s6, 7))):
        sent(src, count, slot)
    own.wait()
    arrived(r6, 7, 19)


def finish(blocks, picked, grad, light):
    for c in range(8):
        grad[:, 32 * c:32 * c + 32, :] = blocks[c].astype(f32)
    for i in range(2):
        light[i] = picked[2 * i:2 * i + 2]


def local(slm_field, target_light):
    T = tables()
    T["tw"] = T["tw"].reshape(2, 8, 1, 256)
    view, lane = np.arange(256) // 16, np.arange(128)
    spread = np.stack([view[:, None] == 4 * g + (lane % 64) // 16 for g in range(4)])
    T["spread"] = spread.astype(jnp.bfloat16)
    T["pick"] = (spread & (lane % 16 == 0) & (lane < 64)).transpose(0, 2, 1).astype(jnp.bfloat16)
    consts = [jnp.asarray(T[k]) for k in NAMES]
    vmem, anywhere = pl.BlockSpec(memory_space=pltpu.VMEM), pl.BlockSpec(memory_space=pl.ANY)
    V = pltpu.VMEM
    block, f_all, b_all = V((8, 2, 32, 256), bf16), V((128, 8, 128), bf16), V((128, 16, 128), bf16)
    line, lines = V((8, 256, 128), bf16), V((8, 256, 128), f32)
    scratch = dict(
        x0=V((2, 256, 256), f32), tv=V((2, 2, 256), f32), x1=block, r1=block, tr=V((8, 2, 2, 256), f32), goals=V((256, 128), f32),
        ra=V((4, 128, 512), bf16), s2=f_all, r2=f_all, xr=V((4, 8, 16, 128), f32), xi=V((4, 8, 16, 128), f32),
        nr=V((2, 4, 8, 16, 128), bf16), ni=V((2, 4, 8, 16, 128), bf16), s3=V((32, 4, 16, 128), bf16), r3=b_all, ps=lines, qs=lines,
        nb=line, jb=line, sp=V((16, 256, 128), f32), bk=V((16, 256, 128), f32), hs=V((4, 512, 256), bf16),
        ls=V((8, 2, 256), f32), lr=V((8, 2, 256), f32), s4=b_all, r4=b_all, od=V((4, 8, 16, 512), f32),
        s5=V((32, 4, 8, 128), bf16), r5=f_all, zr=V((8, 32, 256), f32), zi=V((8, 32, 256), f32), s6=block,
        kr=V((512, 128), f32), ki=V((512, 128), f32),
    )
    blocks, picked = pl.pallas_call(
        body,
        out_shape=(jax.ShapeDtypeStruct((8, 2, 32, 256), bf16), jax.ShapeDtypeStruct((4, 256), f32)),
        in_specs=[anywhere] * (2 + len(NAMES)),
        out_specs=(anywhere, vmem),
        scratch_shapes=[V(T[k].shape, T[k].dtype) for k in NAMES]
        + list(scratch.values())
        + [pltpu.SemaphoreType.DMA((len(NAMES) + 2,)), pltpu.SemaphoreType.DMA((8,)), pltpu.SemaphoreType.DMA((20,))],
        compiler_params=pltpu.CompilerParams(collective_id=0, has_side_effects=True, vmem_limit_bytes=60 << 20),
    )(slm_field, target_light, *consts)
    return pl.pallas_call(
        finish,
        out_shape=(jax.ShapeDtypeStruct((2, 256, 256), f32), jax.ShapeDtypeStruct((2, 2, 256), f32)),
        in_specs=[vmem, vmem],
        out_specs=(vmem, vmem),
    )(blocks, picked)


def solution(mesh):
    return jax.shard_map(
        local,
        mesh=mesh,
        in_specs=(P(None, "rows", "cols"), P("rows", "cols", None)),
        out_specs=(P(None, "rows", "cols"), P("rows", "cols", None)),
        check_vma=False,
    )
```

```python
import math

import jax
import jax.numpy as jnp
import numpy as np
from jax import lax
from jax.experimental import pallas as pl
from jax.experimental.pallas import tpu as pltpu
from jax.sharding import PartitionSpec as P

MESH = pl.DeviceIdType.MESH

f32, bf16 = jnp.float32, jnp.bfloat16

def mm(a, b, dims=((1,), (0,))):
    return lax.dot_general(a, b, (dims, ((), ())), preferred_element_type=f32)

def roll(x, shift):
    return pltpu.roll(x, shift, x.ndim - 1)

def turn(pair, angle):
    re, im = pair
    c, s = math.cos(angle), math.sin(angle)
    if abs(s) < 1e-9:
        return (re, im) if c > 0 else (-re, -im)
    if abs(c) < 1e-9:
        return (-im, re) if s > 0 else (im, -re)
    if abs(abs(c) - abs(s)) < 1e-9:
        k = abs(c)
        a, b = (re, im) if c > 0 else (-re, -im)
        if (s > 0) == (c > 0):
            return k * (a - b), k * (a + b)
        return k * (a + b), k * (b - a)
    return re * c - im * s, re * s + im * c

def fft_list(xs, sign):
    n = len(xs)
    if n == 1:
        return list(xs)
    even, odd = fft_list(xs[0::2], sign), fft_list(xs[1::2], sign)
    out = [None] * n
    for k in range(n // 2):
        t = turn(odd[k], sign * 2 * math.pi * k / n)
        e = even[k]
        out[k] = (e[0] + t[0], e[1] + t[1])
        out[k + n // 2] = (e[0] - t[0], e[1] - t[1])
    return out

def real_fft8(x):
    s = math.sqrt(0.5)
    a0, a1 = x[0] + x[4], x[0] - x[4]
    b0, b1 = x[2] + x[6], x[2] - x[6]
    c0, c1 = x[1] + x[5], x[1] - x[5]
    d0, d1 = x[3] + x[7], x[3] - x[7]
    e1, f1 = s * (c1 - d1), s * (c1 + d1)
    r1, r3 = a1 + e1, a1 - e1
    i1, i3 = -(b1 + f1), b1 - f1
    r2, i2 = a0 - b0, d0 - c0
    p, q = a0 + b0, c0 + d0
    return [(p + q, None), (r1, i1), (r2, i2), (r3, i3), (p - q, None), (r3, -i3), (r2, -i2), (r1, -i1)]

def lane_swap(xs):
    lane = lax.broadcasted_iota(jnp.int32, xs[0].shape, xs[0].ndim - 1)
    for step, (pairs, width) in enumerate((( ((0, 1), (2, 3)), 32), (((0, 2), (1, 3)), 64))):
        low = (lane // width) % 2 == 0
        out = [None] * 4
        for lo, hi in pairs:
            out[lo] = jnp.where(low, xs[lo], roll(xs[hi], width))
            out[hi] = jnp.where(low, roll(xs[lo], 128 - width), xs[hi])
        xs = out
    return xs

def by_i(x):
    lane = lax.broadcasted_iota(jnp.int32, x.shape, x.ndim - 1)
    return jnp.where(lane < 64, -1.0, 1.0) * roll(x, 64)

def tables():
    a = np.arange(256)
    t256 = 2 * np.pi * ((a[:, None] * a[None]) % 256) / 256
    C, S = np.cos(t256), np.sin(t256)
    cs = np.concatenate([C, S], 1)
    b = np.arange(128)
    t128 = 2 * np.pi * ((b[:, None] * b[None]) % 128) / 128
    c1, s1 = np.cos(t128), np.sin(t128)
    dfwd = np.block([[c1, -s1], [s1, c1]])
    dinv = np.block([[c1, s1], [-s1, c1]])
    taper = np.sin(np.pi * (a + 0.5) / 256) ** 2
    tr = taper[:, None] * C
    ti = -taper[:, None] * S
    rr, rim = tr / 256, ti / 256
    row = np.zeros((2, 256, 4, 2, 64))
    for g in range(4):
        s = slice(64 * g, 64 * g + 64)
        row[0, :, g, 0], row[0, :, g, 1] = rr[:, s], rim[:, s]
        row[1, :, g, 0], row[1, :, g, 1] = -rim[:, s], rr[:, s]
    row = row.reshape(512, 512)
    ct = np.concatenate([tr.T, ti.T], 1)
    cth = np.concatenate([tr, ti], 1)
    v0 = np.arange(8)
    th = 2 * np.pi * v0[:, None] * a[None] / 2048
    u0 = np.arange(32)
    t4 = 2 * np.pi * u0[:, None] * b[None] / 4096
    l = np.arange(128)
    ones = ((l[:, None] % 64) // 16 == (l[None] % 64) // 16) / 256.0
    B = lambda x: x.astype(jnp.bfloat16)
    F = lambda x: x.astype(np.float32)
    return dict(cs=B(cs), dfwd=B(dfwd), dinv=B(dinv), row=B(row), rowh=B(row.T.copy()), ct=B(ct), cth=B(cth),
                tw=F(np.stack([np.cos(th), np.sin(th)])),
                twl=F(np.broadcast_to(np.stack([np.cos(th), np.sin(th)])[..., None], (2, 8, 256, 128))),
                t4=F(np.stack([np.cos(t4), np.sin(t4)])), ones=B(ones))

def filt(me):
    q, k = me // 32, me % 32
    u0 = lax.broadcasted_iota(jnp.int32, (32, 16, 128), 0)
    w = lax.broadcasted_iota(jnp.int32, (32, 16, 128), 1)
    u1 = lax.broadcasted_iota(jnp.int32, (32, 16, 128), 2)
    u = 32 * u1 + u0
    v = 8 * (8 * k + w % 8) + 2 * q + w // 8
    fx = jnp.where(u < 2048, u, u - 4096).astype(f32) / 4096
    fy = jnp.where(v < 1024, v, v - 2048).astype(f32) / 2048
    s = fx * fx + fy * fy
    turns = 16000.0 * s / (jnp.sqrt(225.0 - s) + 15.0)
    quarters = 4.0 * (turns - jnp.floor(turns))
    nearest = jnp.floor(quarters + 0.5)
    z = (quarters - nearest) * (math.pi / 2)
    n = nearest.astype(jnp.int32)
    zz = z * z
    sine = z * (1 + zz * (-1 / 6 + zz * (1 / 120 + zz * (-1 / 5040 + zz / 362880))))
    cosine = 1 + zz * (-1 / 2 + zz * (1 / 24 + zz * (-1 / 720 + zz / 40320)))
    odd = n % 2 == 1
    c, d = jnp.where(odd, sine, cosine), jnp.where(odd, cosine, sine)
    half = 2.0 ** -23
    c = jnp.where((n % 4 == 1) | (n % 4 == 2), -half, half) * c
    d = jnp.where(n % 4 >= 2, half, -half) * d
    return c.reshape(512, 128), d.reshape(512, 128)

FAR_FIRST = sorted(
    ((a, b) for a in range(8) for b in range(4)),
    key=lambda p: -(min(p[0] >> 1, 4 - (p[0] >> 1)) + 2 * (p[0] & 1) + min(p[1], 4 - p[1])),
)
QUARTERS = (2, 3, 1, 0)
STEP = 8


def turn_row(table, v):
    return table[0, v], table[1, v]


def columns(xs, T, kr, ki, sign):
    z = fft_list(xs, -1)
    lhs = []
    for u in range(32):
        c, s = T["t4"][0, u:u + 1], T["t4"][1, u:u + 1]
        re, im = z[u]
        lhs.append(jnp.concatenate([re * c + im * s, im * c - re * s], 1).astype(bf16))
    f = mm(jnp.concatenate(lhs, 0), T["dfwd"][...])
    fr, fi = f[:, :128], f[:, 128:]
    if sign > 0:
        pr, pi = fr * kr - fi * ki, fr * ki + fi * kr
    else:
        pr, pi = fr * kr + fi * ki, fi * kr - fr * ki
    g = mm(jnp.concatenate([pr, pi], 1).astype(bf16), T["dinv"][...])
    ys = []
    for u in range(32):
        c, s = T["t4"][0, u:u + 1], T["t4"][1, u:u + 1]
        re, im = g[16 * u:16 * u + 16, :128], g[16 * u:16 * u + 16, 128:]
        ys.append((re * c - im * s, im * c + re * s))
    return fft_list(ys, 1)


def halves(x, table):
    hi = x.astype(bf16)
    return mm(hi, table) + mm((x - hi.astype(f32)).astype(bf16), table)


NAMES = ("tw", "cs", "spread", "t4", "dfwd", "dinv", "row", "twl", "ct", "ones", "cth", "pick", "rowh")


def body(field, target, *refs):
    n = len(NAMES)
    hbm, refs = dict(zip(NAMES, refs[:n])), refs[n:]
    r6, light_out = refs[:2]
    T, refs = dict(zip(NAMES, refs[2:2 + n])), refs[2 + n:]
    (x0, tv, x1, r1, tr, goals, ra, s2, r2, xr, xi, nr, ni, s3, r3, ps, qs, nb, jb, sp, bk, hs, ls, lr, s4, r4, od, s5, r5,
     zr, zi, s6, kr, ki, tsem, ssem, rsem) = refs
    row, col = lax.axis_index("rows"), lax.axis_index("cols")
    z, high, low = 2 * (row & 1) + (col >> 2), row >> 1, col & 3
    me = 32 * z + 4 * high + low
    highs = [((high + (a & 6)) & 6) + ((high + a) & 1) for a in range(8)]
    lows = [(low + b) & 3 for b in range(4)]
    barrier = pltpu.get_barrier_semaphore()
    for k in range(1, 16):
        pl.semaphore_signal(barrier, inc=1, device_id=((row + k) & 15, col), device_id_type=MESH)
    for k in range(1, 8):
        pl.semaphore_signal(barrier, inc=1, device_id=(row, (col + k) & 7), device_id_type=MESH)
    first = [pltpu.make_async_copy(field, x0, tsem.at[n]), pltpu.make_async_copy(target, tv, tsem.at[n + 1])]
    loads = [pltpu.make_async_copy(hbm[k], T[k], tsem.at[i]) for i, k in enumerate(NAMES)]
    for copy in first + loads:
        copy.start()

    def need(*names):
        for k in names:
            loads[NAMES.index(k)].wait()

    def copy_to(src, dst, send, recv, d):
        return pltpu.make_async_remote_copy(src, dst, ssem.at[send], rsem.at[recv], device_id=d, device_id_type=MESH)

    def send_cols(src, dst, send, recv):
        for k in (4, 1, 5, 3, 6, 2, 7):
            d = ((col ^ k) & 4) + ((col + k) & 3)
            copy_to(src(d), dst.at[col], send, recv, (row, d)).start()

    def send_group(src, dst, send, recv, j):
        q = ahead(j)
        up, left = q >> 1, 4 * (q & 1)
        for a, b in FAR_FIRST:
            if a or b or QUARTERS[j]:
                d = 32 * q + 4 * highs[a] + lows[b]
                copy_to(src(d, q, a, b), dst.at[me], send, recv + j, (2 * highs[a] + up, left + lows[b])).start()

    def arrived(dst, count, slot):
        some = dst.at[pl.ds(0, count)]
        copy_to(some, some, 0, slot, (row, col)).wait_recv()

    def sent(src, count, slot):
        some = src.at[pl.ds(0, count)]
        copy_to(some, some, slot, 0, (row, col)).wait_send()

    def ahead(j):
        return z ^ QUARTERS[j]

    def behind(j):
        return z ^ QUARTERS[j]

    for copy in first:
        copy.wait()
    for c in range(8):
        x1[c] = x0[:, 32 * c:32 * c + 32, :].astype(bf16)
    pl.semaphore_wait(barrier, 22)
    send_cols(lambda d: x1.at[d], r1, 0, 0)
    send_cols(lambda d: tv, tr, 1, 1)
    r1[pl.ds(col, 1)] = x1[pl.ds(col, 1)]
    tr[pl.ds(col, 1)] = tv[...][None]
    a, b = filt(me)
    kr[...] = a
    ki[...] = b

    need("tw", "cs")
    arrived(r1, 7, 0)
    zs = fft_list([(r1[c, 0].astype(f32), r1[c, 1].astype(f32)) for c in range(8)], -1)
    for v in range(8):
        q, w = v // 2, 32 * (v % 2)
        c, s = turn_row(T["tw"], v)
        re, im = zs[v]
        if v:
            re, im = re * c + im * s, im * c - re * s
        ra[q, w:w + 32] = jnp.concatenate([re, im], 1).astype(bf16)
        ra[q, 64 + w:96 + w] = jnp.concatenate([im, -re], 1).astype(bf16)
    for j in range(4):
        q = ahead(j)
        y = mm(T["cs"][...], ra[q], ((1,), (1,)))
        s2[pl.ds(32 * q, 32)] = y.reshape(32, 8, 128)
        send_group(lambda d, *_: s2.at[d], r2, 2, 2, j)
        if QUARTERS[j] == 0:
            r2[pl.ds(me, 1)] = s2[pl.ds(me, 1)]

    need("spread")
    arrived(tr, 7, 1)
    lane = lax.broadcasted_iota(jnp.int32, (256, 256), 1) % 16
    which = lax.broadcasted_iota(jnp.int32, (256, 256), 0) % 16
    group = col & 3
    mine = [tr[c, pl.ds(col >> 2, 1)] for c in range(8)]
    rows = [jnp.broadcast_to(mine[j // 2][0, j % 2:j % 2 + 1], (16, 256)) for j in range(16)]
    goals[...] = halves(jnp.where(lane == which, jnp.concatenate(rows, 0), 0.0), T["spread"][group])

    need("t4", "dfwd", "dinv")
    for j in range(4):
        q = behind(j)
        arrived(r2, 32 if QUARTERS[j] else 31, 2 + j)
        x = r2[pl.ds(32 * q, 32)].reshape(8, 4, 8, 128)
        b = lane_swap([x[:, g] for g in range(4)])
        for v in range(2):
            xr[q, :, 8 * v:8 * v + 8] = b[v]
            xi[q, :, 8 * v:8 * v + 8] = b[2 + v]
    xs = [(xr[i % 4, i // 4], xi[i % 4, i // 4]) for i in range(32)]
    for i, (re, im) in enumerate(columns(xs, T, kr[...], ki[...], 1)):
        k = (i - 1) % 32
        for x, part in ((nr, re.astype(bf16)), (ni, im.astype(bf16))):
            x[0, i % 4, i // 4] = part
            x[1, k % 4, k // 4] = part
    need("row")
    for j in range(4):
        q = ahead(j)
        parts = [x[d, q].reshape(128, 128) for x in (nr, ni) for d in range(2)]
        o = mm(jnp.concatenate(parts, 1), T["row"][...])
        for g in range(4):
            s3[pl.ds(8 * q, 8), g] = o[:, 128 * g:128 * g + 128].reshape(8, 16, 128).astype(bf16)
        send_group(lambda d, q, a, b: s3.at[8 * q + highs[a], lows[b]], r3, 3, 6, j)
        if QUARTERS[j] == 0:
            r3[pl.ds(me, 1)] = s3[8 * z + high, pl.ds(low, 1)]

    need("twl", "ct", "ones", "cth", "pick", "rowh")
    for j in range(4):
        q = behind(j)
        arrived(r3, 32 if QUARTERS[j] else 31, 6 + j)
        x = r3[pl.ds(32 * q, 32)].astype(f32).reshape(32, 2, 8, 128)
        cols = []
        for v in range(2):
            xv = x[:, v].reshape(256, 128)
            cols.append(jnp.concatenate([xv.astype(bf16), by_i(xv).astype(bf16)], 0))
        o = mm(T["cs"][...], jnp.concatenate(cols, 1))
        for v in range(2):
            zv = o[:, 128 * v:128 * v + 128]
            ps[2 * q + v] = zv * T["twl"][0, 2 * q + v]
            qs[2 * q + v] = zv * T["twl"][1, 2 * q + v]
    for m in range(0, 256, 32):
        part = slice(m, m + 32)
        for c, (p, q) in enumerate(fft_list([(ps[v, part], qs[v, part]) for v in range(8)], 1)):
            near = p + by_i(q)
            nb[c, part] = near.astype(bf16)
            jb[c, part] = by_i(near).astype(bf16)
    lights = []
    for first in range(0, 8, STEP):
        sums = []
        for c in range(first, first + STEP):
            d = (c + 1) % 8
            even = jnp.concatenate([nb[c], jb[c]], 0)
            odd = jnp.concatenate([nb[c, 128:], nb[d, :128], jb[c, 128:], jb[d, :128]], 0)
            o = mm(T["ct"][...], jnp.concatenate([even, odd], 1))
            for j in range(2):
                s = o[:, 128 * j:128 * j + 128]
                sp[2 * c + j] = s
                sums.append((s * s).reshape(16, 16, 128).sum(1))
        light = halves(jnp.concatenate(sums, 0), T["ones"][...])
        wt = 4.0 * (light - goals[32 * first:32 * first + 32 * STEP])
        lights.append(light)
        for c in range(first, first + STEP):
            cols = []
            for j in (2 * c, 2 * c + 1):
                rows = range(16 * j - 32 * first, 16 * j - 32 * first + 16)
                w = sp[j] * jnp.concatenate([jnp.broadcast_to(wt[r:r + 1], (16, 128)) for r in rows], 0)
                cols.append(jnp.concatenate([w.astype(bf16), (-by_i(w)).astype(bf16)], 0))
            o = mm(T["cth"][...], jnp.concatenate(cols, 1))
            bk[2 * c] = o[:, :128]
            bk[2 * c + 1] = o[:, 128:]
    light = jnp.concatenate(lights, 0)
    for m in range(0, 256, 32):
        part = slice(m, m + 32)
        xs = []
        for c in range(8):
            if m < 128:
                xs.append(bk[2 * c, part] + bk[(2 * c - 1) % 16, m + 128:m + 160])
            else:
                xs.append(bk[2 * c + 1, m - 128:m - 96] + bk[2 * c, part])
        for v, (e, f) in enumerate(real_fft8(xs)):
            c, s = T["twl"][0, v, part], T["twl"][1, v, part]
            if f is None:
                p, q = e * c, -e * s
            else:
                p, q = e * c + f * s, f * c - e * s
            h = p + by_i(q)
            w = slice(128 * (v % 2), 128 * (v % 2) + 128)
            hs[v // 2, part, w] = h.astype(bf16)
            hs[v // 2, 256 + m:288 + m, w] = (-by_i(h)).astype(bf16)
    for j in range(4):
        q = ahead(j)
        y = mm(T["cs"][...], hs[q])
        pair = [y[:, 128 * v:128 * v + 128].reshape(32, 1, 8, 128) for v in range(2)]
        s4[pl.ds(32 * q, 32)] = jnp.concatenate(pair, 1).reshape(32, 16, 128).astype(bf16)
        send_group(lambda d, *_: s4.at[d], r4, 4, 10, j)
        if QUARTERS[j] == 0:
            r4[pl.ds(me, 1)] = s4[pl.ds(me, 1)]
    views = jnp.where(lane == which, halves(light, T["pick"][group]), 0.0).reshape(16, 16, 256).sum(1)
    for c in range(8):
        ls[c] = views[2 * c:2 * c + 2]
    send_cols(lambda d: ls.at[d], lr, 5, 14)
    lr[pl.ds(col, 1)] = ls[pl.ds(col, 1)]

    for j in range(4):
        q = behind(j)
        arrived(r4, 32 if QUARTERS[j] else 31, 10 + j)
        x = r4[pl.ds(32 * q, 32)].reshape(8, 4, 16, 128)
        o = mm(jnp.concatenate([x[:, g].reshape(128, 128) for g in range(4)], 1), T["rowh"][...])
        od[q] = o.reshape(8, 16, 512)
    xs = []
    for i in range(32):
        a, b, k = i % 4, i // 4, (i - 1) % 32
        c, d = k % 4, k // 4
        xs.append((od[a, b, :, :128] + od[c, d, :, 128:256], od[a, b, :, 256:384] + od[c, d, :, 384:]))
    for i, (re, im) in enumerate(columns(xs, T, kr[...], ki[...], -1)):
        xr[i % 4, i // 4] = re
        xi[i % 4, i // 4] = im
    for j in range(4):
        q = ahead(j)
        parts = lane_swap([x[q, :, 8 * v:8 * v + 8] for x in (xr, xi) for v in range(2)])
        for g in range(4):
            s5[pl.ds(8 * q, 8), g] = parts[g]
        send_group(lambda d, q, a, b: s5.at[8 * q + highs[a], lows[b]], r5, 6, 15, j)
        if QUARTERS[j] == 0:
            r5[pl.ds(me, 1)] = s5[8 * z + high, pl.ds(low, 1)]
    arrived(lr, 7, 14)
    for i in range(2):
        light_out[2 * i:2 * i + 2] = (lr[4 * i] + lr[4 * i + 1]) + (lr[4 * i + 2] + lr[4 * i + 3])

    for j in range(4):
        q = behind(j)
        arrived(r5, 32 if QUARTERS[j] else 31, 15 + j)
        x = r5[pl.ds(32 * q, 32)].reshape(256, 128).T.astype(bf16)
        o = mm(x, T["cs"][...])
        for v in range(2):
            pr, pi = o[32 * v:32 * v + 32], o[64 + 32 * v:96 + 32 * v]
            re, im = pr[:, :256] - pi[:, 256:], pi[:, :256] + pr[:, 256:]
            c, s = turn_row(T["tw"], 2 * q + v)
            zr[2 * q + v] = re * c - im * s
            zi[2 * q + v] = im * c + re * s
    for c, (re, im) in enumerate(fft_list([(zr[v], zi[v]) for v in range(8)], 1)):
        s6[c, 0] = re.astype(bf16)
        s6[c, 1] = im.astype(bf16)
    send_cols(lambda d: s6.at[d], r6, 7, 19)
    own = pltpu.make_async_copy(s6.at[col], r6.at[col], tsem.at[0])
    own.start()
    for slot, (src, count) in enumerate(((x1, 7), (tr, 7), (r2, 127), (r3, 127), (r4, 127), (ls, 7), (r5, 127), (s6, 7))):
        sent(src, count, slot)
    own.wait()
    arrived(r6, 7, 19)


def finish(blocks, picked, grad, light):
    for c in range(8):
        grad[:, 32 * c:32 * c + 32, :] = blocks[c].astype(f32)
    for i in range(2):
        light[i] = picked[2 * i:2 * i + 2]


def local(slm_field, target_light):
    T = tables()
    T["tw"] = T["tw"].reshape(2, 8, 1, 256)
    view, lane = np.arange(256) // 16, np.arange(128)
    spread = np.stack([view[:, None] == 4 * g + (lane % 64) // 16 for g in range(4)])
    T["spread"] = spread.astype(jnp.bfloat16)
    T["pick"] = (spread & (lane % 16 == 0) & (lane < 64)).transpose(0, 2, 1).astype(jnp.bfloat16)
    consts = [jnp.asarray(T[k]) for k in NAMES]
    vmem, anywhere = pl.BlockSpec(memory_space=pltpu.VMEM), pl.BlockSpec(memory_space=pl.ANY)
    V = pltpu.VMEM
    block, f_all, b_all = V((8, 2, 32, 256), bf16), V((128, 8, 128), f32), V((128, 16, 128), bf16)
    line, lines = V((8, 256, 128), bf16), V((8, 256, 128), f32)
    scratch = dict(
        x0=V((2, 256, 256), f32), tv=V((2, 2, 256), f32), x1=block, r1=block, tr=V((8, 2, 2, 256), f32), goals=V((256, 128), f32),
        ra=V((4, 128, 512), bf16), s2=f_all, r2=f_all, xr=V((4, 8, 16, 128), f32), xi=V((4, 8, 16, 128), f32),
        nr=V((2, 4, 8, 16, 128), bf16), ni=V((2, 4, 8, 16, 128), bf16), s3=V((32, 4, 16, 128), bf16), r3=b_all, ps=lines, qs=lines,
        nb=line, jb=line, sp=V((16, 256, 128), f32), bk=V((16, 256, 128), f32), hs=V((4, 512, 256), bf16),
        ls=V((8, 2, 256), f32), lr=V((8, 2, 256), f32), s4=b_all, r4=b_all, od=V((4, 8, 16, 512), f32),
        s5=V((32, 4, 8, 128), f32), r5=f_all, zr=V((8, 32, 256), f32), zi=V((8, 32, 256), f32), s6=block,
        kr=V((512, 128), f32), ki=V((512, 128), f32),
    )
    blocks, picked = pl.pallas_call(
        body,
        out_shape=(jax.ShapeDtypeStruct((8, 2, 32, 256), bf16), jax.ShapeDtypeStruct((4, 256), f32)),
        in_specs=[anywhere] * (2 + len(NAMES)),
        out_specs=(anywhere, vmem),
        scratch_shapes=[V(T[k].shape, T[k].dtype) for k in NAMES]
        + list(scratch.values())
        + [pltpu.SemaphoreType.DMA((len(NAMES) + 2,)), pltpu.SemaphoreType.DMA((8,)), pltpu.SemaphoreType.DMA((20,))],
        compiler_params=pltpu.CompilerParams(collective_id=0, has_side_effects=True, vmem_limit_bytes=60 << 20),
    )(slm_field, target_light, *consts)
    return pl.pallas_call(
        finish,
        out_shape=(jax.ShapeDtypeStruct((2, 256, 256), f32), jax.ShapeDtypeStruct((2, 2, 256), f32)),
        in_specs=[vmem, vmem],
        out_specs=(vmem, vmem),
    )(blocks, picked)


def solution(mesh):
    return jax.shard_map(
        local,
        mesh=mesh,
        in_specs=(P(None, "rows", "cols"), P("rows", "cols", None)),
        out_specs=(P(None, "rows", "cols"), P("rows", "cols", None)),
        check_vma=False,
    )
```

```python
import math

import jax
import jax.numpy as jnp
import numpy as np
from jax import lax
from jax.experimental import pallas as pl
from jax.experimental.pallas import tpu as pltpu
from jax.sharding import PartitionSpec as P

MESH = pl.DeviceIdType.MESH

f32, bf16 = jnp.float32, jnp.bfloat16

def mm(a, b, dims=((1,), (0,))):
    return lax.dot_general(a, b, (dims, ((), ())), preferred_element_type=f32)

def roll(x, shift):
    return pltpu.roll(x, shift, x.ndim - 1)

def turn(pair, angle):
    re, im = pair
    c, s = math.cos(angle), math.sin(angle)
    if abs(s) < 1e-9:
        return (re, im) if c > 0 else (-re, -im)
    if abs(c) < 1e-9:
        return (-im, re) if s > 0 else (im, -re)
    if abs(abs(c) - abs(s)) < 1e-9:
        k = abs(c)
        a, b = (re, im) if c > 0 else (-re, -im)
        if (s > 0) == (c > 0):
            return k * (a - b), k * (a + b)
        return k * (a + b), k * (b - a)
    return re * c - im * s, re * s + im * c

def fft_list(xs, sign):
    n = len(xs)
    if n == 1:
        return list(xs)
    even, odd = fft_list(xs[0::2], sign), fft_list(xs[1::2], sign)
    out = [None] * n
    for k in range(n // 2):
        t = turn(odd[k], sign * 2 * math.pi * k / n)
        e = even[k]
        out[k] = (e[0] + t[0], e[1] + t[1])
        out[k + n // 2] = (e[0] - t[0], e[1] - t[1])
    return out

def real_fft8(x):
    s = math.sqrt(0.5)
    a0, a1 = x[0] + x[4], x[0] - x[4]
    b0, b1 = x[2] + x[6], x[2] - x[6]
    c0, c1 = x[1] + x[5], x[1] - x[5]
    d0, d1 = x[3] + x[7], x[3] - x[7]
    e1, f1 = s * (c1 - d1), s * (c1 + d1)
    r1, r3 = a1 + e1, a1 - e1
    i1, i3 = -(b1 + f1), b1 - f1
    r2, i2 = a0 - b0, d0 - c0
    p, q = a0 + b0, c0 + d0
    return [(p + q, None), (r1, i1), (r2, i2), (r3, i3), (p - q, None), (r3, -i3), (r2, -i2), (r1, -i1)]

def lane_swap(xs):
    lane = lax.broadcasted_iota(jnp.int32, xs[0].shape, xs[0].ndim - 1)
    for step, (pairs, width) in enumerate((( ((0, 1), (2, 3)), 32), (((0, 2), (1, 3)), 64))):
        low = (lane // width) % 2 == 0
        out = [None] * 4
        for lo, hi in pairs:
            out[lo] = jnp.where(low, xs[lo], roll(xs[hi], width))
            out[hi] = jnp.where(low, roll(xs[lo], 128 - width), xs[hi])
        xs = out
    return xs

def by_i(x):
    lane = lax.broadcasted_iota(jnp.int32, x.shape, x.ndim - 1)
    return jnp.where(lane < 64, -1.0, 1.0) * roll(x, 64)

def tables():
    a = np.arange(256)
    t256 = 2 * np.pi * ((a[:, None] * a[None]) % 256) / 256
    C, S = np.cos(t256), np.sin(t256)
    cs = np.concatenate([C, S], 1)
    b = np.arange(128)
    t128 = 2 * np.pi * ((b[:, None] * b[None]) % 128) / 128
    c1, s1 = np.cos(t128), np.sin(t128)
    dfwd = np.block([[c1, -s1], [s1, c1]])
    dinv = np.block([[c1, s1], [-s1, c1]])
    taper = np.sin(np.pi * (a + 0.5) / 256) ** 2
    tr = taper[:, None] * C
    ti = -taper[:, None] * S
    rr, rim = tr / 256, ti / 256
    row = np.zeros((2, 256, 4, 2, 64))
    for g in range(4):
        s = slice(64 * g, 64 * g + 64)
        row[0, :, g, 0], row[0, :, g, 1] = rr[:, s], rim[:, s]
        row[1, :, g, 0], row[1, :, g, 1] = -rim[:, s], rr[:, s]
    row = row.reshape(512, 512)
    ct = np.concatenate([tr.T, ti.T], 1)
    cth = np.concatenate([tr, ti], 1)
    v0 = np.arange(8)
    th = 2 * np.pi * v0[:, None] * a[None] / 2048
    u0 = np.arange(32)
    t4 = 2 * np.pi * u0[:, None] * b[None] / 4096
    l = np.arange(128)
    ones = ((l[:, None] % 64) // 16 == (l[None] % 64) // 16) / 256.0
    B = lambda x: x.astype(jnp.bfloat16)
    F = lambda x: x.astype(np.float32)
    return dict(cs=B(cs), dfwd=B(dfwd), dinv=B(dinv), row=B(row), rowh=B(row.T.copy()), ct=B(ct), cth=B(cth),
                tw=F(np.stack([np.cos(th), np.sin(th)])),
                twl=F(np.broadcast_to(np.stack([np.cos(th), np.sin(th)])[..., None], (2, 8, 256, 128))),
                t4=F(np.stack([np.cos(t4), np.sin(t4)])), ones=B(ones))

def filt(me):
    q, k = me // 32, me % 32
    u0 = lax.broadcasted_iota(jnp.int32, (32, 16, 128), 0)
    w = lax.broadcasted_iota(jnp.int32, (32, 16, 128), 1)
    u1 = lax.broadcasted_iota(jnp.int32, (32, 16, 128), 2)
    u = 32 * u1 + u0
    v = 8 * (8 * k + w % 8) + 2 * q + w // 8
    fx = jnp.where(u < 2048, u, u - 4096).astype(f32) / 4096
    fy = jnp.where(v < 1024, v, v - 2048).astype(f32) / 2048
    s = fx * fx + fy * fy
    turns = 16000.0 * s / (jnp.sqrt(225.0 - s) + 15.0)
    quarters = 4.0 * (turns - jnp.floor(turns))
    nearest = jnp.floor(quarters + 0.5)
    z = (quarters - nearest) * (math.pi / 2)
    n = nearest.astype(jnp.int32)
    zz = z * z
    sine = z * (1 + zz * (-1 / 6 + zz * (1 / 120 + zz * (-1 / 5040 + zz / 362880))))
    cosine = 1 + zz * (-1 / 2 + zz * (1 / 24 + zz * (-1 / 720 + zz / 40320)))
    odd = n % 2 == 1
    c, d = jnp.where(odd, sine, cosine), jnp.where(odd, cosine, sine)
    half = 2.0 ** -23
    c = jnp.where((n % 4 == 1) | (n % 4 == 2), -half, half) * c
    d = jnp.where(n % 4 >= 2, half, -half) * d
    return c.reshape(512, 128), d.reshape(512, 128)

FAR_FIRST = sorted(
    ((a, b) for a in range(8) for b in range(4)),
    key=lambda p: (-min(p[0] >> 1, 4 - (p[0] >> 1)), -2 * (p[0] & 1) - min(p[1], 4 - p[1])),
)
QUARTERS = (2, 3, 1, 0)
STEP = 8


def turn_row(table, v):
    return table[0, v], table[1, v]


def columns(xs, T, kr, ki, sign):
    z = fft_list(xs, -1)
    lhs = []
    for u in range(32):
        c, s = T["t4"][0, u:u + 1], T["t4"][1, u:u + 1]
        re, im = z[u]
        lhs.append(jnp.concatenate([re * c + im * s, im * c - re * s], 1).astype(bf16))
    f = mm(jnp.concatenate(lhs, 0), T["dfwd"][...])
    fr, fi = f[:, :128], f[:, 128:]
    if sign > 0:
        pr, pi = fr * kr - fi * ki, fr * ki + fi * kr
    else:
        pr, pi = fr * kr + fi * ki, fi * kr - fr * ki
    g = mm(jnp.concatenate([pr, pi], 1).astype(bf16), T["dinv"][...])
    ys = []
    for u in range(32):
        c, s = T["t4"][0, u:u + 1], T["t4"][1, u:u + 1]
        re, im = g[16 * u:16 * u + 16, :128], g[16 * u:16 * u + 16, 128:]
        ys.append((re * c - im * s, im * c + re * s))
    return fft_list(ys, 1)


def halves(x, table):
    hi = x.astype(bf16)
    return mm(hi, table) + mm((x - hi.astype(f32)).astype(bf16), table)


NAMES = ("tw", "cs", "spread", "t4", "dfwd", "dinv", "row", "twl", "ct", "ones", "cth", "pick", "rowh")


def body(field, target, *refs):
    n = len(NAMES)
    hbm, refs = dict(zip(NAMES, refs[:n])), refs[n:]
    r6, light_out = refs[:2]
    T, refs = dict(zip(NAMES, refs[2:2 + n])), refs[2 + n:]
    (x0, tv, x1, r1, tr, goals, ra, s2, r2, xr, xi, nr, ni, s3, r3, ps, qs, nb, jb, sp, bk, hs, ls, lr, s4, r4, od, s5, r5,
     zr, zi, s6, kr, ki, tsem, ssem, rsem) = refs
    row, col = lax.axis_index("rows"), lax.axis_index("cols")
    z, high, low = 2 * (row & 1) + (col >> 2), row >> 1, col & 3
    me = 32 * z + 4 * high + low
    highs = [((high + (a & 6)) & 6) + ((high + a) & 1) for a in range(8)]
    lows = [(low + b) & 3 for b in range(4)]
    barrier = pltpu.get_barrier_semaphore()
    for k in range(1, 16):
        pl.semaphore_signal(barrier, inc=1, device_id=((row + k) & 15, col), device_id_type=MESH)
    for k in range(1, 8):
        pl.semaphore_signal(barrier, inc=1, device_id=(row, (col + k) & 7), device_id_type=MESH)
    first = [pltpu.make_async_copy(field, x0, tsem.at[n]), pltpu.make_async_copy(target, tv, tsem.at[n + 1])]
    loads = [pltpu.make_async_copy(hbm[k], T[k], tsem.at[i]) for i, k in enumerate(NAMES)]
    for copy in first + loads:
        copy.start()

    def need(*names):
        for k in names:
            loads[NAMES.index(k)].wait()

    def copy_to(src, dst, send, recv, d):
        return pltpu.make_async_remote_copy(src, dst, ssem.at[send], rsem.at[recv], device_id=d, device_id_type=MESH)

    def send_cols(src, dst, send, recv):
        for k in (4, 1, 5, 3, 6, 2, 7):
            d = ((col ^ k) & 4) + ((col + k) & 3)
            copy_to(src(d), dst.at[col], send, recv, (row, d)).start()

    def send_group(src, dst, send, recv, j):
        q = ahead(j)
        up, left = q >> 1, 4 * (q & 1)
        for a, b in FAR_FIRST:
            if a or b or QUARTERS[j]:
                d = 32 * q + 4 * highs[a] + lows[b]
                copy_to(src(d, q, a, b), dst.at[me], send, recv + j, (2 * highs[a] + up, left + lows[b])).start()

    def arrived(dst, count, slot):
        some = dst.at[pl.ds(0, count)]
        copy_to(some, some, 0, slot, (row, col)).wait_recv()

    def sent(src, count, slot):
        some = src.at[pl.ds(0, count)]
        copy_to(some, some, slot, 0, (row, col)).wait_send()

    def ahead(j):
        return z ^ QUARTERS[j]

    def behind(j):
        return z ^ QUARTERS[j]

    for copy in first:
        copy.wait()
    for c in range(8):
        x1[c] = x0[:, 32 * c:32 * c + 32, :].astype(bf16)
    pl.semaphore_wait(barrier, 22)
    send_cols(lambda d: x1.at[d], r1, 0, 0)
    send_cols(lambda d: tv, tr, 1, 1)
    r1[pl.ds(col, 1)] = x1[pl.ds(col, 1)]
    tr[pl.ds(col, 1)] = tv[...][None]
    a, b = filt(me)
    kr[...] = a
    ki[...] = b

    need("tw", "cs")
    arrived(r1, 7, 0)
    zs = fft_list([(r1[c, 0].astype(f32), r1[c, 1].astype(f32)) for c in range(8)], -1)
    for v in range(8):
        q, w = v // 2, 32 * (v % 2)
        c, s = turn_row(T["tw"], v)
        re, im = zs[v]
        if v:
            re, im = re * c + im * s, im * c - re * s
        ra[q, w:w + 32] = jnp.concatenate([re, im], 1).astype(bf16)
        ra[q, 64 + w:96 + w] = jnp.concatenate([im, -re], 1).astype(bf16)
    for j in range(4):
        q = ahead(j)
        y = mm(T["cs"][...], ra[q], ((1,), (1,)))
        s2[pl.ds(32 * q, 32)] = y.reshape(32, 8, 128).astype(bf16)
        send_group(lambda d, *_: s2.at[d], r2, 2, 2, j)
        if QUARTERS[j] == 0:
            r2[pl.ds(me, 1)] = s2[pl.ds(me, 1)]

    need("spread")
    arrived(tr, 7, 1)
    lane = lax.broadcasted_iota(jnp.int32, (256, 256), 1) % 16
    which = lax.broadcasted_iota(jnp.int32, (256, 256), 0) % 16
    group = col & 3
    mine = [tr[c, pl.ds(col >> 2, 1)] for c in range(8)]
    rows = [jnp.broadcast_to(mine[j // 2][0, j % 2:j % 2 + 1], (16, 256)) for j in range(16)]
    goals[...] = halves(jnp.where(lane == which, jnp.concatenate(rows, 0), 0.0), T["spread"][group])

    need("t4", "dfwd", "dinv")
    for j in range(4):
        q = behind(j)
        arrived(r2, 32 if QUARTERS[j] else 31, 2 + j)
        x = r2[pl.ds(32 * q, 32)].astype(f32).reshape(8, 4, 8, 128)
        b = lane_swap([x[:, g] for g in range(4)])
        for v in range(2):
            xr[q, :, 8 * v:8 * v + 8] = b[v]
            xi[q, :, 8 * v:8 * v + 8] = b[2 + v]
    xs = [(xr[i % 4, i // 4], xi[i % 4, i // 4]) for i in range(32)]
    for i, (re, im) in enumerate(columns(xs, T, kr[...], ki[...], 1)):
        k = (i - 1) % 32
        for x, part in ((nr, re.astype(bf16)), (ni, im.astype(bf16))):
            x[0, i % 4, i // 4] = part
            x[1, k % 4, k // 4] = part
    need("row")
    for j in range(4):
        q = ahead(j)
        parts = [x[d, q].reshape(128, 128) for x in (nr, ni) for d in range(2)]
        o = mm(jnp.concatenate(parts, 1), T["row"][...])
        for g in range(4):
            s3[pl.ds(8 * q, 8), g] = o[:, 128 * g:128 * g + 128].reshape(8, 16, 128).astype(bf16)
        send_group(lambda d, q, a, b: s3.at[8 * q + highs[a], lows[b]], r3, 3, 6, j)
        if QUARTERS[j] == 0:
            r3[pl.ds(me, 1)] = s3[8 * z + high, pl.ds(low, 1)]

    need("twl", "ct", "ones", "cth", "pick", "rowh")
    for j in range(4):
        q = behind(j)
        arrived(r3, 32 if QUARTERS[j] else 31, 6 + j)
        x = r3[pl.ds(32 * q, 32)].astype(f32).reshape(32, 2, 8, 128)
        cols = []
        for v in range(2):
            xv = x[:, v].reshape(256, 128)
            cols.append(jnp.concatenate([xv.astype(bf16), by_i(xv).astype(bf16)], 0))
        o = mm(T["cs"][...], jnp.concatenate(cols, 1))
        for v in range(2):
            zv = o[:, 128 * v:128 * v + 128]
            ps[2 * q + v] = zv * T["twl"][0, 2 * q + v]
            qs[2 * q + v] = zv * T["twl"][1, 2 * q + v]
    for m in range(0, 256, 32):
        part = slice(m, m + 32)
        for c, (p, q) in enumerate(fft_list([(ps[v, part], qs[v, part]) for v in range(8)], 1)):
            near = p + by_i(q)
            nb[c, part] = near.astype(bf16)
            jb[c, part] = by_i(near).astype(bf16)
    lights = []
    for first in range(0, 8, STEP):
        sums = []
        for c in range(first, first + STEP):
            d = (c + 1) % 8
            even = jnp.concatenate([nb[c], jb[c]], 0)
            odd = jnp.concatenate([nb[c, 128:], nb[d, :128], jb[c, 128:], jb[d, :128]], 0)
            o = mm(T["ct"][...], jnp.concatenate([even, odd], 1))
            for j in range(2):
                s = o[:, 128 * j:128 * j + 128]
                sp[2 * c + j] = s
                sums.append((s * s).reshape(16, 16, 128).sum(1))
        light = halves(jnp.concatenate(sums, 0), T["ones"][...])
        wt = 4.0 * (light - goals[32 * first:32 * first + 32 * STEP])
        lights.append(light)
        for c in range(first, first + STEP):
            cols = []
            for j in (2 * c, 2 * c + 1):
                rows = range(16 * j - 32 * first, 16 * j - 32 * first + 16)
                w = sp[j] * jnp.concatenate([jnp.broadcast_to(wt[r:r + 1], (16, 128)) for r in rows], 0)
                cols.append(jnp.concatenate([w.astype(bf16), (-by_i(w)).astype(bf16)], 0))
            o = mm(T["cth"][...], jnp.concatenate(cols, 1))
            bk[2 * c] = o[:, :128]
            bk[2 * c + 1] = o[:, 128:]
    light = jnp.concatenate(lights, 0)
    for m in range(0, 256, 32):
        part = slice(m, m + 32)
        xs = []
        for c in range(8):
            if m < 128:
                xs.append(bk[2 * c, part] + bk[(2 * c - 1) % 16, m + 128:m + 160])
            else:
                xs.append(bk[2 * c + 1, m - 128:m - 96] + bk[2 * c, part])
        for v, (e, f) in enumerate(real_fft8(xs)):
            c, s = T["twl"][0, v, part], T["twl"][1, v, part]
            if f is None:
                p, q = e * c, -e * s
            else:
                p, q = e * c + f * s, f * c - e * s
            h = p + by_i(q)
            w = slice(128 * (v % 2), 128 * (v % 2) + 128)
            hs[v // 2, part, w] = h.astype(bf16)
            hs[v // 2, 256 + m:288 + m, w] = (-by_i(h)).astype(bf16)
    for j in range(4):
        q = ahead(j)
        y = mm(T["cs"][...], hs[q])
        pair = [y[:, 128 * v:128 * v + 128].reshape(32, 1, 8, 128) for v in range(2)]
        s4[pl.ds(32 * q, 32)] = jnp.concatenate(pair, 1).reshape(32, 16, 128).astype(bf16)
        send_group(lambda d, *_: s4.at[d], r4, 4, 10, j)
        if QUARTERS[j] == 0:
            r4[pl.ds(me, 1)] = s4[pl.ds(me, 1)]
    views = jnp.where(lane == which, halves(light, T["pick"][group]), 0.0).reshape(16, 16, 256).sum(1)
    for c in range(8):
        ls[c] = views[2 * c:2 * c + 2]
    send_cols(lambda d: ls.at[d], lr, 5, 14)
    lr[pl.ds(col, 1)] = ls[pl.ds(col, 1)]

    for j in range(4):
        q = behind(j)
        arrived(r4, 32 if QUARTERS[j] else 31, 10 + j)
        x = r4[pl.ds(32 * q, 32)].reshape(8, 4, 16, 128)
        o = mm(jnp.concatenate([x[:, g].reshape(128, 128) for g in range(4)], 1), T["rowh"][...])
        od[q] = o.reshape(8, 16, 512)
    xs = []
    for i in range(32):
        a, b, k = i % 4, i // 4, (i - 1) % 32
        c, d = k % 4, k // 4
        xs.append((od[a, b, :, :128] + od[c, d, :, 128:256], od[a, b, :, 256:384] + od[c, d, :, 384:]))
    for i, (re, im) in enumerate(columns(xs, T, kr[...], ki[...], -1)):
        xr[i % 4, i // 4] = re
        xi[i % 4, i // 4] = im
    for j in range(4):
        q = ahead(j)
        parts = lane_swap([x[q, :, 8 * v:8 * v + 8] for x in (xr, xi) for v in range(2)])
        for g in range(4):
            s5[pl.ds(8 * q, 8), g] = parts[g].astype(bf16)
        send_group(lambda d, q, a, b: s5.at[8 * q + highs[a], lows[b]], r5, 6, 15, j)
        if QUARTERS[j] == 0:
            r5[pl.ds(me, 1)] = s5[8 * z + high, pl.ds(low, 1)]
    arrived(lr, 7, 14)
    for i in range(2):
        light_out[2 * i:2 * i + 2] = (lr[4 * i] + lr[4 * i + 1]) + (lr[4 * i + 2] + lr[4 * i + 3])

    for j in range(4):
        q = behind(j)
        arrived(r5, 32 if QUARTERS[j] else 31, 15 + j)
        x = r5[pl.ds(32 * q, 32)].astype(f32).reshape(256, 128).T.astype(bf16)
        o = mm(x, T["cs"][...])
        for v in range(2):
            pr, pi = o[32 * v:32 * v + 32], o[64 + 32 * v:96 + 32 * v]
            re, im = pr[:, :256] - pi[:, 256:], pi[:, :256] + pr[:, 256:]
            c, s = turn_row(T["tw"], 2 * q + v)
            zr[2 * q + v] = re * c - im * s
            zi[2 * q + v] = im * c + re * s
    blocks = fft_list([(zr[v], zi[v]) for v in range(8)], 1)
    for half in range(2):
        for c in range(8):
            s6[c, half] = blocks[c][half].astype(bf16)
        for k in (4, 1, 5, 3, 6, 2, 7):
            d = ((col ^ k) & 4) + ((col + k) & 3)
            copy_to(s6.at[d, half], r6.at[col, half], 7, 19, (row, d)).start()
    own = pltpu.make_async_copy(s6.at[col], r6.at[col], tsem.at[0])
    own.start()
    for slot, (src, count) in enumerate(((x1, 7), (tr, 7), (r2, 127), (r3, 127), (r4, 127), (ls, 7), (r5, 127), (s6, 7))):
        sent(src, count, slot)
    own.wait()
    arrived(r6, 7, 19)


def finish(blocks, picked, grad, light):
    for c in range(8):
        grad[:, 32 * c:32 * c + 32, :] = blocks[c].astype(f32)
    for i in range(2):
        light[i] = picked[2 * i:2 * i + 2]


def local(slm_field, target_light):
    T = tables()
    T["tw"] = T["tw"].reshape(2, 8, 1, 256)
    view, lane = np.arange(256) // 16, np.arange(128)
    spread = np.stack([view[:, None] == 4 * g + (lane % 64) // 16 for g in range(4)])
    T["spread"] = spread.astype(jnp.bfloat16)
    T["pick"] = (spread & (lane % 16 == 0) & (lane < 64)).transpose(0, 2, 1).astype(jnp.bfloat16)
    consts = [jnp.asarray(T[k]) for k in NAMES]
    vmem, anywhere = pl.BlockSpec(memory_space=pltpu.VMEM), pl.BlockSpec(memory_space=pl.ANY)
    V = pltpu.VMEM
    block, f_all, b_all = V((8, 2, 32, 256), bf16), V((128, 8, 128), bf16), V((128, 16, 128), bf16)
    line, lines = V((8, 256, 128), bf16), V((8, 256, 128), f32)
    scratch = dict(
        x0=V((2, 256, 256), f32), tv=V((2, 2, 256), f32), x1=block, r1=block, tr=V((8, 2, 2, 256), f32), goals=V((256, 128), f32),
        ra=V((4, 128, 512), bf16), s2=f_all, r2=f_all, xr=V((4, 8, 16, 128), f32), xi=V((4, 8, 16, 128), f32),
        nr=V((2, 4, 8, 16, 128), bf16), ni=V((2, 4, 8, 16, 128), bf16), s3=V((32, 4, 16, 128), bf16), r3=b_all, ps=lines, qs=lines,
        nb=line, jb=line, sp=V((16, 256, 128), f32), bk=V((16, 256, 128), f32), hs=V((4, 512, 256), bf16),
        ls=V((8, 2, 256), f32), lr=V((8, 2, 256), f32), s4=b_all, r4=b_all, od=V((4, 8, 16, 512), f32),
        s5=V((32, 4, 8, 128), bf16), r5=f_all, zr=V((8, 32, 256), f32), zi=V((8, 32, 256), f32), s6=block,
        kr=V((512, 128), f32), ki=V((512, 128), f32),
    )
    blocks, picked = pl.pallas_call(
        body,
        out_shape=(jax.ShapeDtypeStruct((8, 2, 32, 256), bf16), jax.ShapeDtypeStruct((4, 256), f32)),
        in_specs=[anywhere] * (2 + len(NAMES)),
        out_specs=(anywhere, vmem),
        scratch_shapes=[V(T[k].shape, T[k].dtype) for k in NAMES]
        + list(scratch.values())
        + [pltpu.SemaphoreType.DMA((len(NAMES) + 2,)), pltpu.SemaphoreType.DMA((8,)), pltpu.SemaphoreType.DMA((20,))],
        compiler_params=pltpu.CompilerParams(collective_id=0, has_side_effects=True, vmem_limit_bytes=60 << 20),
    )(slm_field, target_light, *consts)
    return pl.pallas_call(
        finish,
        out_shape=(jax.ShapeDtypeStruct((2, 256, 256), f32), jax.ShapeDtypeStruct((2, 2, 256), f32)),
        in_specs=[vmem, vmem],
        out_specs=(vmem, vmem),
    )(blocks, picked)


def solution(mesh):
    return jax.shard_map(
        local,
        mesh=mesh,
        in_specs=(P(None, "rows", "cols"), P("rows", "cols", None)),
        out_specs=(P(None, "rows", "cols"), P("rows", "cols", None)),
        check_vma=False,
    )
```
